256 devices in a mesh: ctx: 32 (over x, z), head: 8 (over y, core).
Axes of the slice: x: 4, y: 4, z: 8, core: 2. Of those that a mesh axis runs over, the one named last changes fastest.
Arguments:
- signal: bfloat16 [49152, 5120], P(('ctx', 'head')), may hold values from -0.125 to 0.125
- cotangent: bfloat16 [49152, 5120], P(('ctx', 'head')), may hold values from -0.125 to 0.125
- input_map: bfloat16 [49152, 128], P('ctx'), may hold values from -1.75 to 1.75
- output_map: bfloat16 [49152, 128], P('ctx'), may hold values from -1.75 to 1.75
- log_decay: float32 [49152, 80], P('ctx', 'head'), may hold values from -1 to 0, as said below
- skip_gain: float32 [80], P('head'), may hold values from 0.5 to 2
Outputs:
- scan_out: bfloat16 [49152, 5120], P(('ctx', 'head'))
- grad_signal: bfloat16 [49152, 5120], P(('ctx', 'head'))
- grad_input_map: float32 [49152, 128], P('ctx')
- grad_output_map: float32 [49152, 128], P('ctx')
- grad_decay: float32 [49152, 80], P('ctx', 'head')
The draws below stay inside these ranges and needn't reach their ends.
Inputs may be any that keep to these rules, and one draw needn't show every extreme that they name: `log_decay`: every entry is negative.
All inputs are finite; a program needn't handle non-finite values.
Results may differ from the reference program's by a relative error of at most 0.0027.
Values may be sent and summed in bfloat16 or wider, within the bound.
No kernel may reach another device: no remote copies, remote signals or barrier semaphores. Data moves between devices by JAX's collectives and lax.ppermute only.
A program may use at most 192 MiB of HBM per device.

```python
import math
import jax
import jax.numpy as jnp
from jax import lax

H = 80
STATE = 128
GROUP_POSITIONS = 256
INNER = 5120
CTX_LEN = 1536
SEQUENCE_TOKENS = 49152
N_CTX = 32


def draw_log_decay(key, part):
    random_keys = jax.random.split(key, 7)
    kinds = jax.random.randint(random_keys[0], (H,), 0, 4)
    fast_heads = kinds >= 2
    slow_rate = jnp.exp(jax.random.uniform(random_keys[1], (H,), minval=math.log(0.0001), maxval=math.log(0.001)))
    fast_rate = jnp.exp(jax.random.uniform(random_keys[2], (H,), minval=math.log(1.0 / 50.0), maxval=math.log(1.0 / 30.0)))
    baseline_rate = jnp.where(fast_heads, fast_rate, slow_rate)
    block_count = SEQUENCE_TOKENS // CTX_LEN
    block_multiplier = jnp.exp(jax.random.uniform(random_keys[3], (block_count, H), minval=math.log(0.6), maxval=math.log(1.4)))
    block_multiplier = jnp.repeat(block_multiplier, CTX_LEN, axis=0)
    surface_jitter = jax.random.uniform(random_keys[4], (SEQUENCE_TOKENS, H), minval=0.5, maxval=1.5)
    spike_count = max(SEQUENCE_TOKENS // (4 * GROUP_POSITIONS), 3)
    token_positions = jax.random.randint(random_keys[5], (spike_count,), 0, SEQUENCE_TOKENS)
    loss_values = jax.random.uniform(random_keys[6], (spike_count,), minval=0.2, maxval=0.35)
    device_places = jnp.arange(SEQUENCE_TOKENS)
    spike_events = jnp.sum(jnp.where(device_places[:, None] == token_positions[None, :], jnp.log1p(-loss_values)[None, :], 0.0), axis=1)
    value_rows = -baseline_rate[None, :] * block_multiplier * surface_jitter + spike_events[:, None]
    return value_rows.astype(jnp.float32)


def levels(own_key, shape, cuts, low, top_value):
    level, own = 1.0, jax.random.fold_in(own_key, 6)
    for position, shards_of in cuts:
        heights = jnp.exp(jax.random.uniform(jax.random.fold_in(own, position), (shards_of,), jnp.float32, low / len(cuts), top_value / len(cuts)))
        level = level * jnp.repeat(heights, shape[position] // shards_of).reshape([-1 if axis == position else 1 for axis in range(len(shape))])
    return level


def scatter_about(stream_key, dims, scale, limit, cuts=(), held_as=jnp.bfloat16):
    values = jax.random.normal(stream_key, dims, jnp.float32) * scale
    if len(cuts) > 0:
        values = levels(stream_key, dims, cuts, -0.22, 0.18) * values
    return jnp.clip(values, min=-limit, max=limit).astype(held_as)


def setup_inputs(seed: int = 0) -> dict:
    keys = jax.random.split(jax.random.key(seed), 7)
    signal = scatter_about(keys[0], (SEQUENCE_TOKENS, INNER), 0.02, 0.125, ((0, 256),))
    cotangent = scatter_about(keys[1], (SEQUENCE_TOKENS, INNER), 0.02, 0.125, ((0, 256),))
    input_map = scatter_about(keys[2], (SEQUENCE_TOKENS, STATE), 0.3, 1.75, ((0, 32),))
    output_map = scatter_about(keys[3], (SEQUENCE_TOKENS, STATE), 0.3, 1.75, ((0, 32),))
    log_decay = draw_log_decay(jax.random.fold_in(keys[6], 71), 0)
    skip_gain = jnp.clip(0.5 + 1.5 * jax.random.uniform(keys[5], (H,), jnp.float32) ** levels(keys[5], (H,), ((0, 8),), -0.2, 0.2), 0.5, 2.0)
    return {"signal": signal, "cotangent": cotangent, "input_map": input_map, "output_map": output_map, "log_decay": log_decay, "skip_gain": skip_gain}


exact_mode = lax.Precision.HIGHEST

def decay_tables(log_decay, group_len):
    length, head_count = log_decay.shape
    groups = length // group_len
    inside = jnp.cumsum(log_decay.reshape(groups, group_len, head_count), axis=1)
    totals = inside[:, -1, :]
    across = jnp.cumsum(totals, axis=0)
    return (inside, totals, across, across - totals)

def local_block(signal_full, inputs_full, outputs_full, log_decay, skip_gain, group_len):
    length, head_count = log_decay.shape
    groups = length // group_len
    inside, totals, across, before = decay_tables(log_decay, group_len)
    signal_blocks = signal_full.reshape(groups, group_len, head_count, -1)
    inputs_blocks = inputs_full.reshape(groups, group_len, -1)
    outputs_blocks = outputs_full.reshape(groups, group_len, -1)
    scores = jnp.einsum('cin,cjn->cij', outputs_blocks, inputs_blocks, precision=exact_mode)
    by_head = jnp.swapaxes(inside, 1, 2)
    causal = lax.broadcasted_iota(jnp.int32, (group_len, group_len), 0) >= lax.broadcasted_iota(jnp.int32, (group_len, group_len), 1)
    differences = jnp.where(causal, by_head[:, :, :, None] - by_head[:, :, None, :], 0.0)
    decays = jnp.where(causal, jnp.exp(differences), 0.0)
    weights = lax.optimization_barrier((scores[:, None, :, :] * decays).astype(jnp.bfloat16)).astype(jnp.float32)
    within = jnp.einsum('chij,cjhp->cihp', weights, signal_blocks, precision=exact_mode)
    to_end = jnp.exp(totals[:, None, :] - inside)
    states = jnp.einsum('cqhp,cqn->chpn', signal_blocks * to_end[..., None], inputs_blocks, precision=exact_mode)
    later_mask = lax.broadcasted_iota(jnp.int32, (groups, groups), 0) > lax.broadcasted_iota(jnp.int32, (groups, groups), 1)
    spans_log = jnp.where(later_mask[:, :, None], before[:, None, :] - across[None, :, :], 0.0)
    carry_weights = jnp.where(later_mask[:, :, None], jnp.exp(spans_log), 0.0)
    entering = jnp.einsum('kch,chpn->khpn', carry_weights, states, precision=exact_mode)
    carried_in = jnp.einsum('cqn,chpn->cqhp', outputs_blocks, entering, precision=exact_mode) * jnp.exp(inside)[..., None]
    combined = within + carried_in + skip_gain[None, None, :, None] * signal_blocks
    closing = jnp.einsum('ch,chpn->hpn', jnp.exp(across[-1][None, :] - across), states, precision=exact_mode)
    return (combined.reshape(length, -1), closing)

def carried_part(outputs_full, log_decay, incoming):
    length, head_count = log_decay.shape
    running = jnp.cumsum(log_decay, axis=0)
    portion = jnp.einsum('tn,hpn->thp', outputs_full, incoming, precision=exact_mode) * jnp.exp(running)[..., None]
    return (portion.reshape(length, -1), jnp.exp(running[-1])[:, None, None] * incoming)

def backward_seed(tangent_full, outputs_full, log_decay):
    length, head_count = log_decay.shape
    running = jnp.cumsum(log_decay, axis=0)
    weighted = tangent_full.reshape(length, head_count, -1) * jnp.exp(running)[..., None]
    return jnp.einsum('thp,tn->hpn', weighted, outputs_full, precision=exact_mode)

def reference(signal, cotangent, input_map, output_map, log_decay, skip_gain):
    blocks = N_CTX
    block_len = SEQUENCE_TOKENS // N_CTX
    signal_all = signal.astype(jnp.float32).reshape(blocks, block_len, -1)
    tangent_all = cotangent.astype(jnp.float32).reshape(blocks, block_len, -1)
    inputs_all = input_map.astype(jnp.float32).reshape(blocks, block_len, -1)
    outputs_all = output_map.astype(jnp.float32).reshape(blocks, block_len, -1)
    decay_all = log_decay.reshape(blocks, block_len, -1)

    def first_pass(pieces):
        signal_full, tangent_full, inputs_full, outputs_full, decay_full = pieces
        closing = local_block(signal_full, inputs_full, outputs_full, decay_full, skip_gain, GROUP_POSITIONS)[1]
        retained = jnp.exp(jnp.cumsum(decay_full, axis=0)[-1])
        return (closing, retained, backward_seed(tangent_full, outputs_full, decay_full))
    closings, retains, seeds = lax.map(first_pass, (signal_all, tangent_all, inputs_all, outputs_all, decay_all))

    def chain_step(carry, pieces):
        retained, addition = pieces
        return (retained[:, None, None] * carry + addition, carry)
    zero_state = jnp.zeros_like(closings[0])
    final_fwd, enterings = lax.scan(chain_step, zero_state, (retains, closings))
    final_bwd, leavings = lax.scan(chain_step, zero_state, (retains, seeds), reverse=True)

    def second_pass(pieces):
        signal_full, tangent_full, inputs_full, outputs_full, decay_full, entering, leaving = pieces

        def own_part(signal_part, inputs_part, outputs_part, decay_part):
            return local_block(signal_part, inputs_part, outputs_part, decay_part, skip_gain, GROUP_POSITIONS)
        (own_out, own_state), own_pull = jax.vjp(own_part, signal_full, inputs_full, outputs_full, decay_full)
        (carried, passed), carry_pull = jax.vjp(carried_part, outputs_full, decay_full, entering)
        combined = (own_out + carried).astype(jnp.bfloat16)
        grad_sig, grad_in, grad_out_a, grad_decay_a = own_pull((tangent_full, leaving))
        grad_out_b, grad_decay_b, unused = carry_pull((tangent_full, leaving))
        return (combined, grad_sig.astype(jnp.bfloat16), grad_in, grad_out_a + grad_out_b, grad_decay_a + grad_decay_b)
    results = lax.map(second_pass, (signal_all, tangent_all, inputs_all, outputs_all, decay_all, enterings, leavings))
    scan_out = results[0].reshape(SEQUENCE_TOKENS, -1)
    grad_signal = results[1].reshape(SEQUENCE_TOKENS, -1)
    grad_input_map = results[2].reshape(SEQUENCE_TOKENS, -1)
    grad_output_map = results[3].reshape(SEQUENCE_TOKENS, -1)
    grad_decay = results[4].reshape(SEQUENCE_TOKENS, -1)
    return (scan_out, grad_signal, grad_input_map, grad_output_map, grad_decay)
```

```python
import jax
import jax.numpy as jnp
from jax import lax
from jax.experimental import pallas as pl
from jax.experimental.pallas import tpu as pltpu
from jax.sharding import Mesh
from jax.sharding import PartitionSpec as P

ROWS = 192
N = 128
HEAD = 64
HG = 10
GC = HG * HEAD
GROUPS = 8
PAIRS = GC // 128
F32, BF16 = jnp.float32, jnp.bfloat16
SWAP = [(0, 1), (1, 0)]
NN = (((1,), (0,)), ((), ()))
NT = (((1,), (1,)), ((), ()))
TN = (((0,), (0,)), ((), ()))


def dot(a, b, dims=NN):
    return lax.dot_general(a, b, dims, preferred_element_type=F32)


def halves(v):
    high = v.astype(BF16)
    return high, (v - high.astype(F32)).astype(BF16)


def thirds(v):
    high = v.astype(BF16)
    rest = v - high.astype(F32)
    middle = rest.astype(BF16)
    return high, middle, (rest - middle.astype(F32)).astype(BF16)


def spread(columns):
    rows = columns.shape[0]
    first = lax.broadcasted_iota(jnp.int32, (rows, 128), 1) < HEAD
    return jnp.concatenate(
        [
            jnp.where(
                first,
                jnp.broadcast_to(columns[:, 2 * p : 2 * p + 1], (rows, 128)),
                jnp.broadcast_to(columns[:, 2 * p + 1 : 2 * p + 2], (rows, 128)),
            )
            for p in range(PAIRS)
        ],
        axis=1,
    )


def states_kernel(core, x_ref, dy_ref, cum_ref, bt_ref, ct_ref, s_ref, g_ref):
    cum = cum_ref[0]
    to_end = jnp.exp(cum[ROWS - 1 : ROWS, :] - cum)
    high, low = halves(x_ref[...].astype(F32) * spread(to_end))
    bt = bt_ref[...]
    s_ref[0, 0] = dot(bt, high) + dot(bt, low)
    high, low = halves(dy_ref[...].astype(F32) * spread(jnp.exp(cum)))
    ct = ct_ref[...]
    g_ref[0, 0] = dot(ct, high) + dot(ct, low)


def local_states(core, x, dy, cum, bt, ct):
    def group(s, core):
        return 2 * (s % 4) + (core[0] + 1 + s // 4) % 2

    state = jax.ShapeDtypeStruct((2, 4, N, GC), F32)
    whole = lambda s, core: (0, 0)
    return pl.pallas_call(
        states_kernel,
        grid_spec=pltpu.PrefetchScalarGridSpec(
            num_scalar_prefetch=1,
            grid=(GROUPS,),
            in_specs=[
                pl.BlockSpec((ROWS, GC), lambda s, core: (0, group(s, core))),
                pl.BlockSpec((ROWS, GC), lambda s, core: (0, group(s, core))),
                pl.BlockSpec((1, ROWS, 16), lambda s, core: (group(s, core), 0, 0)),
                pl.BlockSpec((N, ROWS), whole),
                pl.BlockSpec((N, ROWS), whole),
            ],
            out_specs=[
                pl.BlockSpec((1, 1, N, GC), lambda s, core: (s // 4, s % 4, 0, 0)),
                pl.BlockSpec((1, 1, N, GC), lambda s, core: (s // 4, s % 4, 0, 0)),
            ],
        ),
        out_shape=[state, state],
        compiler_params=pltpu.CompilerParams(vmem_limit_bytes=40 << 20),
        name="local_states",
    )(core, x, dy, cum, bt, ct)


def within_kernel(
    x_ref, dy_ref, cum_ref, cumt_ref, b_ref, c_ref, y_ref, dx_ref, db_ref, dc_ref, score_ref, acc_ref
):
    step = pl.program_id(0)
    causal = lax.broadcasted_iota(jnp.int32, (ROWS, ROWS), 0) >= lax.broadcasted_iota(
        jnp.int32, (ROWS, ROWS), 1
    )

    @pl.when(step == 0)
    def _():
        score_ref[...] = jnp.where(causal, dot(c_ref[...], b_ref[...], NT), 0.0)
        acc_ref[...] = jnp.zeros_like(acc_ref)

    first = lax.broadcasted_iota(jnp.int32, (ROWS, 128), 1) < HEAD
    zero = jnp.zeros((ROWS, 128), BF16)
    for p in range(PAIRS):
        columns = slice(128 * p, 128 * p + 128)
        x = x_ref[:, columns]
        dy = dy_ref[:, columns]
        y = dx = None
        for side in range(2):
            h = 2 * p + side
            keep = first if side == 0 else jnp.logical_not(first)
            xs = jnp.where(keep, x, zero)
            dys = jnp.where(keep, dy, zero)
            decay = jnp.exp(
                jnp.minimum(cum_ref[0, :, h : h + 1] - cumt_ref[0, h : h + 1, :], 0.0)
            )
            weights = (score_ref[...] * decay).astype(BF16)
            part = dot(weights, xs)
            y = part if y is None else y + part
            dweights = dot(dys, x, NT).astype(BF16).astype(F32)
            acc_ref[...] += dweights * decay
            part = dot(weights, dys, TN)
            dx = part if dx is None else dx + part
        y_ref[:, columns] = y
        dx_ref[:, columns] = dx

    @pl.when(step == GROUPS - 1)
    def _():
        high, low = halves(jnp.where(causal, acc_ref[...], 0.0))
        b, c = b_ref[...], c_ref[...]
        dc_ref[...] = dot(high, b) + dot(low, b)
        db_ref[...] = dot(high, c, TN) + dot(low, c, TN)


def within(x, dy, cum, cumt, b, c):
    by_column = pl.BlockSpec((ROWS, GC), lambda s: (0, s))
    whole = pl.BlockSpec((ROWS, N), lambda s: (0, 0))
    wide = jax.ShapeDtypeStruct((ROWS, GC * GROUPS), F32)
    small = jax.ShapeDtypeStruct((ROWS, N), F32)
    return pl.pallas_call(
        within_kernel,
        grid=(GROUPS,),
        in_specs=[
            by_column,
            by_column,
            pl.BlockSpec((1, ROWS, 16), lambda s: (s, 0, 0)),
            pl.BlockSpec((1, 16, ROWS), lambda s: (s, 0, 0)),
            whole,
            whole,
        ],
        out_specs=[by_column, by_column, whole, whole],
        out_shape=[wide, wide, small, small],
        scratch_shapes=[pltpu.VMEM((ROWS, ROWS), F32), pltpu.VMEM((ROWS, ROWS), F32)],
        compiler_params=pltpu.CompilerParams(vmem_limit_bytes=40 << 20),
        cost_estimate=pl.CostEstimate(
            flops=20_000_000_000, bytes_accessed=12_000_000, transcendentals=3_000_000
        ),
        name="within_chunk",
    )(x, dy, cum, cumt, b, c)


def finish_kernel(
    core, x_ref, dy_ref, cum_ref, cumt_ref, y_ref, dx_ref, ekeep_ref, ecome_ref, gkeep_ref, gcome_ref,
    gain_ref, b_ref, c_ref, db0_ref, dc0_ref, out_ref, gs_ref, db_ref, dc_ref, gd_ref,
):
    step = pl.program_id(0)

    @pl.when(step == 0)
    def _():
        db_ref[...] = db0_ref[...]
        dc_ref[...] = dc0_ref[...]

    kept = step < 4
    entering = jnp.where(kept, ekeep_ref[0], ecome_ref[0])
    leaving = jnp.where(kept, gkeep_ref[0], gcome_ref[0])
    cum = cum_ref[0]
    from_start = spread(jnp.exp(cum))
    to_end = spread(jnp.exp(cum[ROWS - 1 : ROWS, :] - cum))
    x = x_ref[...].astype(F32)
    dy = dy_ref[...].astype(F32)
    gain = gain_ref[0]
    b, c = b_ref[...], c_ref[...]
    e_high, e_low = halves(entering)
    y = y_ref[...] + from_start * (dot(c, e_high) + dot(c, e_low))
    out_ref[...] = (y + gain * x).astype(BF16)
    g_high, g_low = halves(leaving)
    dx_in = dx_ref[...]
    dx_carried = to_end * (dot(b, g_high) + dot(b, g_low))
    gs_ref[...] = (dx_in + dx_carried + gain * dy).astype(BF16)
    high, low = halves(from_start * dy)
    dc_ref[...] += dot(high, e_high, NT) + dot(high, e_low, NT) + dot(low, e_high, NT)
    high, low = halves(to_end * x)
    db_ref[...] += dot(high, g_high, NT) + dot(high, g_low, NT) + dot(low, g_high, NT)
    of_head = (
        lax.broadcasted_iota(jnp.int32, (16, GC), 1) // HEAD
        == lax.broadcasted_iota(jnp.int32, (16, GC), 0)
    ).astype(BF16)

    def by_head(v):
        high, low = halves(v)
        return dot(of_head, high, NT) + dot(of_head, low, NT)

    here = by_head(dy * y - x * dx_in)
    carried = by_head(x * dx_carried)
    across = by_head(
        jnp.broadcast_to(jnp.sum(entering * leaving, axis=0, keepdims=True), (ROWS, GC))
    )
    t = lax.broadcasted_iota(jnp.int32, (ROWS, ROWS), 0)
    s = lax.broadcasted_iota(jnp.int32, (ROWS, ROWS), 1)
    after = (t >= s).astype(BF16)
    before = (t < s).astype(BF16)
    gd = across * jnp.exp(cumt_ref[0, :, ROWS - 1 : ROWS])
    for part in thirds(here):
        gd += dot(part, after)
    for part in thirds(carried):
        gd += dot(part, before)
    gd_ref[0] = gd


def finish(core, x, dy, cum, cumt, y, dx, ekeep, ecome, gkeep, gcome, gain, b, c, db, dc):
    def group(s, core):
        return 2 * (s % 4) + (core[0] + s // 4) % 2

    by_column = pl.BlockSpec((ROWS, GC), lambda s, core: (0, group(s, core)))
    by_group = lambda *shape: pl.BlockSpec(
        (1, *shape), lambda s, core: (group(s, core), *(0 for _ in shape))
    )
    kept = pl.BlockSpec((1, N, GC), lambda s, core: (jnp.minimum(s, 3), 0, 0))
    come = pl.BlockSpec((1, N, GC), lambda s, core: (jnp.maximum(s - 4, 0), 0, 0))
    whole = pl.BlockSpec((ROWS, N), lambda s, core: (0, 0))
    narrow = jax.ShapeDtypeStruct((ROWS, GC * GROUPS), BF16)
    small = jax.ShapeDtypeStruct((ROWS, N), F32)
    return pl.pallas_call(
        finish_kernel,
        grid_spec=pltpu.PrefetchScalarGridSpec(
            num_scalar_prefetch=1,
            grid=(GROUPS,),
            in_specs=[
                by_column, by_column, by_group(ROWS, 16), by_group(16, ROWS), by_column, by_column,
                kept, come, kept, come, by_group(1, GC), whole, whole, whole, whole,
            ],
            out_specs=[by_column, by_column, whole, whole, by_group(16, ROWS)],
        ),
        out_shape=[narrow, narrow, small, small, jax.ShapeDtypeStruct((GROUPS, 16, ROWS), F32)],
        compiler_params=pltpu.CompilerParams(vmem_limit_bytes=48 << 20),
        name="finish",
    )(core, x, dy, cum, cumt, y, dx, ekeep, ecome, gkeep, gcome, gain, b, c, db, dc)


def totals_kernel(s_ref, g_ref, d_ref, tile_ref, out_ref):
    d = [d_ref[i : i + 1, :] for i in range(4)]
    f = ((s_ref[0] * d[1] + s_ref[1]) * d[2] + s_ref[2]) * d[3] + s_ref[3]
    g = ((g_ref[3] * d[2] + g_ref[2]) * d[1] + g_ref[1]) * d[0] + g_ref[0]
    out_ref[0:16, :, 0:GC] = f.reshape(16, 8, GC)
    out_ref[16:32, :, 0:GC] = g.reshape(16, 8, GC)
    out_ref[:, :, GC:] = jnp.broadcast_to(tile_ref[...][None], (32, 8, 128))


def chain_kernel(flag_ref, p_ref, out_ref):
    backward = flag_ref[0]
    state = [jnp.zeros((8, 128), F32) for _ in range(PAIRS)]
    for s in range(32):
        k = jnp.where(backward == 1, 31 - s, s)
        for t in range(PAIRS):
            columns = slice(128 * t, 128 * t + 128)
            out_ref[k, :, columns] = state[t]
            state[t] = state[t] * p_ref[k, t : t + 1, GC:] + p_ref[k, :, columns]


def entering_kernel(s_ref, g_ref, d_ref, edge_ref, e_ref, l_ref):
    d = [d_ref[i : i + 1, :] for i in range(4)]
    e = edge_ref[0:16].reshape(N, GC)
    for i in range(4):
        e_ref[i] = e
        if i < 3:
            e = e * d[i] + s_ref[i]
    g = edge_ref[16:32].reshape(N, GC)
    for i in (3, 2, 1, 0):
        l_ref[i] = g
        if i > 0:
            g = g * d[i] + g_ref[i]


VMEM = pl.BlockSpec(memory_space=pltpu.VMEM)
SMEM = pl.BlockSpec(memory_space=pltpu.SMEM)
ROOM = pltpu.CompilerParams(vmem_limit_bytes=40 << 20)


def shards(x, dy, b_all, c_all, log_decay, skip_gain):
    ix, iz = lax.axis_index("x"), lax.axis_index("z")
    iy, core = lax.axis_index("y"), lax.axis_index("core")
    core_arr = core.reshape(1).astype(jnp.int32)
    row0 = (2 * iy + core) * ROWS
    b = lax.dynamic_slice_in_dim(b_all, row0, ROWS, 0)
    c = lax.dynamic_slice_in_dim(c_all, row0, ROWS, 0)

    by_row = log_decay.T.reshape(HG, 4, 2, ROWS).transpose(1, 2, 0, 3)
    by_row = jnp.concatenate(
        [
            by_row,
            jnp.broadcast_to(jnp.pad(skip_gain, (0, ROWS - HG)), (4, 2, 1, ROWS)),
            jnp.zeros((4, 2, 5, ROWS), F32),
        ],
        axis=2,
    )
    send = jnp.broadcast_to(by_row[:, None], (4, 2, 2, 16, ROWS)).reshape(GROUPS, 2, 16, ROWS)
    got = lax.all_to_all(send, ("y", "core"), split_axis=0, concat_axis=0, tiled=True)
    gain = jnp.repeat(got[:, 0, HG, :HG], HEAD, axis=1).reshape(GROUPS, 1, GC)
    decays = jnp.where(lax.broadcasted_iota(jnp.int32, got.shape, 2) < HG, got, 0.0)
    own = lax.dynamic_index_in_dim(decays, core, 1, keepdims=False)
    upper = jnp.triu(jnp.ones((ROWS, ROWS), F32))
    cumt = lax.dot_general(
        own, upper, (((2,), (0,)), ((), ())), precision=lax.Precision.HIGHEST
    )
    cum = jnp.swapaxes(cumt, 1, 2)
    both = jnp.sum(decays[:, :, :HG], axis=3).reshape(4, 2, 2, HG)
    both = lax.dynamic_index_in_dim(both, core, 1, keepdims=False)
    kept = jnp.repeat(jnp.exp(both), HEAD, axis=2)[:, :, None, :]
    of_chip = jnp.sum(log_decay.reshape(4, 2 * ROWS, HG), axis=1)
    chip_keep = jnp.repeat(jnp.exp(of_chip), HEAD, axis=1)
    tile = jnp.repeat(jnp.exp(jnp.sum(of_chip, axis=0)), HEAD).reshape(PAIRS, 128)
    tile = jnp.pad(tile, ((0, 8 - PAIRS), (0, 0)))

    s_local, g_local = local_states(core_arr, x, dy, cum, b.T, c.T)
    s_come = lax.ppermute(s_local[0], "core", SWAP)
    g_come = lax.ppermute(g_local[0], "core", SWAP)
    s_mine, g_mine = s_local[1], g_local[1]
    low = core == 0
    s0, s1 = jnp.where(low, s_mine, s_come), jnp.where(low, s_come, s_mine)
    g0, g1 = jnp.where(low, g_mine, g_come), jnp.where(low, g_come, g_mine)
    s_chip = kept[:, 1] * s0 + s1
    g_chip = g0 + kept[:, 0] * g1
    exchange = lambda v: lax.all_to_all(v, "y", split_axis=0, concat_axis=0, tiled=True)
    s_all, g_all = exchange(s_chip), exchange(g_chip)
    y_in, dx_in, db_in, dc_in = within(x, dy, cum, cumt, b, c)

    payload = pl.pallas_call(
        totals_kernel,
        in_specs=[VMEM] * 4,
        out_specs=VMEM,
        out_shape=jax.ShapeDtypeStruct((32, 8, GC + 128), F32),
        compiler_params=ROOM,
        name="group_totals",
    )(s_all, g_all, chip_keep, tile)
    payload = lax.all_to_all(payload, ("x", "z"), split_axis=0, concat_axis=0, tiled=True)
    edges = pl.pallas_call(
        chain_kernel,
        in_specs=[SMEM, VMEM],
        out_specs=VMEM,
        out_shape=jax.ShapeDtypeStruct((32, 8, GC), F32),
        compiler_params=ROOM,
        name="chain",
    )((ix >= 2).reshape(1).astype(jnp.int32), payload)
    edges = lax.all_to_all(edges, ("x", "z"), split_axis=0, concat_axis=0, tiled=True)
    e_all, l_all = pl.pallas_call(
        entering_kernel,
        in_specs=[VMEM] * 4,
        out_specs=[VMEM] * 2,
        out_shape=[jax.ShapeDtypeStruct((4, N, GC), F32)] * 2,
        compiler_params=ROOM,
        name="entering",
    )(s_all, g_all, chip_keep, edges)
    e_chip, l_chip = exchange(e_all), exchange(l_all)
    e_late = kept[:, 0] * e_chip + s0
    l_early = kept[:, 1] * l_chip + g1
    e_keep, e_send = jnp.where(low, e_chip, e_late), jnp.where(low, e_late, e_chip)
    l_keep, l_send = jnp.where(low, l_early, l_chip), jnp.where(low, l_chip, l_early)
    e_come = lax.ppermute(e_send, "core", SWAP)
    l_come = lax.ppermute(l_send, "core", SWAP)
    out, grad_x, db, dc, gd = finish(
        core_arr, x, dy, cum, cumt, y_in, dx_in, e_keep, e_come, l_keep, l_come, gain, b, c, db_in, dc_in
    )

    gd = lax.all_to_all(gd, ("y", "core"), split_axis=0, concat_axis=0, tiled=True)
    grad_decay = gd[:, :HG].transpose(0, 2, 1).reshape(GROUPS * ROWS, HG)
    maps = jnp.concatenate([db, dc], axis=1)
    turns = [maps] + [
        lax.ppermute(maps, "y", [(i, (i - s) % 4) for i in range(4)]) for s in (1, 2, 3)
    ]
    chips = jnp.roll(jnp.stack(turns), iy, axis=0)
    other = lax.ppermute(chips, "core", SWAP)
    whole = jnp.stack(
        [jnp.where(low, chips, other), jnp.where(low, other, chips)], axis=1
    ).reshape(GROUPS * ROWS, 2 * N)
    return out, grad_x, whole[:, :N], whole[:, N:], grad_decay


def solution(mesh):
    grid = Mesh(mesh.devices.reshape(4, 8, 4, 2), ("x", "z", "y", "core"))
    ctx, head = ("x", "z"), ("y", "core")
    rows = P((*ctx, *head), None)
    return jax.shard_map(
        shards,
        mesh=grid,
        in_specs=(rows, rows, P(ctx, None), P(ctx, None), P(ctx, head), P(head)),
        out_specs=(rows, rows, P(ctx, None), P(ctx, None), P(ctx, head)),
        check_vma=False,
    )
```

```python
import functools

import jax
import jax.numpy as jnp
from jax import lax
from jax.experimental import pallas as pl
from jax.experimental.pallas import tpu as pltpu
from jax.sharding import Mesh
from jax.sharding import PartitionSpec as P

ROWS = 192
N = 128
HEAD = 64
HG = 10
GC = HG * HEAD
GROUPS = 8
PAIRS = GC // 128
F32, BF16 = jnp.float32, jnp.bfloat16
SWAP = [(0, 1), (1, 0)]
NN = (((1,), (0,)), ((), ()))
NT = (((1,), (1,)), ((), ()))
TN = (((0,), (0,)), ((), ()))


def dot(a, b, dims=NN):
    return lax.dot_general(a, b, dims, preferred_element_type=F32)


def halves(v):
    high = v.astype(BF16)
    return high, (v - high.astype(F32)).astype(BF16)


def thirds(v):
    high = v.astype(BF16)
    rest = v - high.astype(F32)
    middle = rest.astype(BF16)
    return high, middle, (rest - middle.astype(F32)).astype(BF16)


def spread(columns):
    rows = columns.shape[0]
    first = lax.broadcasted_iota(jnp.int32, (rows, 128), 1) < HEAD
    return jnp.concatenate(
        [
            jnp.where(
                first,
                jnp.broadcast_to(columns[:, 2 * p : 2 * p + 1], (rows, 128)),
                jnp.broadcast_to(columns[:, 2 * p + 1 : 2 * p + 2], (rows, 128)),
            )
            for p in range(PAIRS)
        ],
        axis=1,
    )


def within_kernel(
    x_ref, dy_ref, cum_ref, cumt_ref, b_ref, c_ref, y_ref, dx_ref, db_ref, dc_ref, score_ref, acc_ref
):
    step = pl.program_id(0)
    causal = lax.broadcasted_iota(jnp.int32, (ROWS, ROWS), 0) >= lax.broadcasted_iota(
        jnp.int32, (ROWS, ROWS), 1
    )

    @pl.when(step == 0)
    def _():
        score_ref[...] = jnp.where(causal, dot(c_ref[...], b_ref[...], NT), 0.0)
        acc_ref[...] = jnp.zeros_like(acc_ref)

    first = lax.broadcasted_iota(jnp.int32, (ROWS, 128), 1) < HEAD
    zero = jnp.zeros((ROWS, 128), BF16)
    for p in range(PAIRS):
        columns = slice(128 * p, 128 * p + 128)
        x = x_ref[:, columns]
        dy = dy_ref[:, columns]
        y = dx = None
        for side in range(2):
            h = 2 * p + side
            keep = first if side == 0 else jnp.logical_not(first)
            xs = jnp.where(keep, x, zero)
            dys = jnp.where(keep, dy, zero)
            decay = jnp.exp(
                jnp.minimum(cum_ref[0, :, h : h + 1] - cumt_ref[0, h : h + 1, :], 0.0)
            )
            weights = (score_ref[...] * decay).astype(BF16)
            part = dot(weights, xs)
            y = part if y is None else y + part
            dweights = dot(dys, x, NT).astype(BF16).astype(F32)
            acc_ref[...] += dweights * decay
            part = dot(weights, dys, TN)
            dx = part if dx is None else dx + part
        y_ref[:, columns] = y
        dx_ref[:, columns] = dx

    @pl.when(step == GROUPS - 1)
    def _():
        high, low = halves(jnp.where(causal, acc_ref[...], 0.0))
        b, c = b_ref[...], c_ref[...]
        dc_ref[...] = dot(high, b) + dot(low, b)
        db_ref[...] = dot(high, c, TN) + dot(low, c, TN)


def within(x, dy, cum, cumt, b, c):
    by_column = pl.BlockSpec((ROWS, GC), lambda s: (0, s))
    whole = pl.BlockSpec((ROWS, N), lambda s: (0, 0))
    wide = jax.ShapeDtypeStruct((ROWS, GC * GROUPS), F32)
    small = jax.ShapeDtypeStruct((ROWS, N), F32)
    return pl.pallas_call(
        within_kernel,
        grid=(GROUPS,),
        in_specs=[
            by_column,
            by_column,
            pl.BlockSpec((1, ROWS, 16), lambda s: (s, 0, 0)),
            pl.BlockSpec((1, 16, ROWS), lambda s: (s, 0, 0)),
            whole,
            whole,
        ],
        out_specs=[by_column, by_column, whole, whole],
        out_shape=[wide, wide, small, small],
        scratch_shapes=[pltpu.VMEM((ROWS, ROWS), F32), pltpu.VMEM((ROWS, ROWS), F32)],
        compiler_params=pltpu.CompilerParams(vmem_limit_bytes=40 << 20),
        cost_estimate=pl.CostEstimate(
            flops=20_000_000_000, bytes_accessed=12_000_000, transcendentals=3_000_000
        ),
        name="within_chunk",
    )(x, dy, cum, cumt, b, c)


CHIPS = 4
VMEM = pl.BlockSpec(memory_space=pltpu.VMEM)
SMEM = pl.BlockSpec(memory_space=pltpu.SMEM)
PAIR = (2, N, GC)
RETURN = F32


def on_chip(kernel, name, outs, *args, scratch=(), scalars=1):
    return pl.pallas_call(
        kernel,
        in_specs=[SMEM] * scalars + [VMEM] * (len(args) - scalars),
        out_specs=[VMEM] * len(outs),
        out_shape=outs,
        scratch_shapes=list(scratch),
        compiler_params=pltpu.CompilerParams(vmem_limit_bytes=44 << 20),
        name=name,
    )(*args)


def pack_kernel(ld_ref, gain_ref, out_ref):
    out_ref[...] = jnp.zeros_like(out_ref)
    for chunk in range(GROUPS):
        rows = ld_ref[:, chunk * ROWS : (chunk + 1) * ROWS]
        for core in range(2):
            at = 2 * (chunk // 2) + core
            out_ref[at, chunk % 2, 0:HG, :] = rows
            out_ref[at, chunk % 2, HG : HG + 1, 0:HG] = gain_ref[...]


def owner_kernel(ld_ref, out_ref):
    width = 2 * ROWS
    of = lax.broadcasted_iota(jnp.int32, (8, 8 * ROWS), 1) // width
    row = lax.broadcasted_iota(jnp.int32, (8, 8 * ROWS), 0)
    pick = jnp.logical_or(of == row, row == CHIPS).astype(BF16)
    totals = sum(dot(pick, part, NT) for part in thirds(ld_ref[...]))
    out_ref[...] = spread(jnp.exp(totals))


def decays_kernel(core_ref, got_ref, cumt_ref, cum_ref, gain_ref, kept_ref):
    low = core_ref[0] == 0
    t = lax.broadcasted_iota(jnp.int32, (ROWS, ROWS), 0)
    s = lax.broadcasted_iota(jnp.int32, (ROWS, ROWS), 1)
    upper = (t <= s).astype(BF16)
    lower = (t >= s).astype(BF16)
    is_head = lax.broadcasted_iota(jnp.int32, (GROUPS, 16, ROWS), 1) < HG
    flat, tall = [], []
    for half in range(2):
        ld = jnp.where(is_head, got_ref[:, half], 0.0).reshape(GROUPS * 16, ROWS)
        parts = thirds(ld)
        flat.append(sum(dot(part, upper) for part in parts))
        tall.append(sum(dot(lower, part, NT) for part in parts))
    cumt_ref[...] = jnp.where(low, flat[0], flat[1]).reshape(GROUPS, 16, ROWS)
    own = jnp.where(low, tall[0], tall[1])
    for g in range(GROUPS):
        cum_ref[g] = own[:, 16 * g : 16 * g + 16]
        gain_ref[g] = spread(got_ref[g, 0, HG : HG + 1, :])
    for half in range(2):
        ends = jnp.exp(tall[half][ROWS - 1 : ROWS, :])
        for j in range(CHIPS):
            a = ends[:, 32 * j : 32 * j + 16]
            b = ends[:, 32 * j + 16 : 32 * j + 32]
            kept_ref[half, j] = spread(jnp.where(low, a, b))


def states_kernel(place, x_ref, dy_ref, cum_ref, bt_ref, ct_ref, send_ref, keep_ref):
    low = place[0] == 0
    for way, (v_ref, m_ref) in enumerate(((x_ref, bt_ref), (dy_ref, ct_ref))):
        m = m_ref[...]
        states = []
        for k in range(2):
            cum = cum_ref[k]
            scale = jnp.exp(cum[ROWS - 1 : ROWS, :] - cum if way == 0 else cum)
            high, low_part = halves(v_ref[:, k * GC : (k + 1) * GC].astype(F32) * spread(scale))
            states.append(dot(m, high) + dot(m, low_part))
        keep_ref[0, way] = jnp.where(low, states[0], states[1])
        send_ref[0, way] = jnp.where(low, states[1], states[0])


def chunk_states(place, x, dy, cum, bt, ct):
    columns = pl.BlockSpec((ROWS, 2 * GC), lambda s, place: (0, s))
    whole = pl.BlockSpec((N, ROWS), lambda s, place: (0, 0))
    quad = pl.BlockSpec((1, *PAIR), lambda s, place: (s, 0, 0, 0))
    return pl.pallas_call(
        states_kernel,
        grid_spec=pltpu.PrefetchScalarGridSpec(
            num_scalar_prefetch=1,
            grid=(CHIPS,),
            in_specs=[
                columns,
                columns,
                pl.BlockSpec((2, ROWS, 16), lambda s, place: (s, 0, 0)),
                whole,
                whole,
            ],
            out_specs=[quad, quad],
        ),
        out_shape=[jax.ShapeDtypeStruct((CHIPS, *PAIR), F32)] * 2,
        compiler_params=pltpu.CompilerParams(vmem_limit_bytes=60 << 20),
        name="chunk_states",
    )(place, x, dy, cum, bt, ct)


def join_kernel(place_ref, keep_ref, come_ref, kept_ref, *outs):
    low = place_ref[0] == 0
    for turn, out in enumerate(outs):
        j = lax.rem(place_ref[1] + turn, CHIPS)
        for way in range(2):
            scaled = low if way == 0 else jnp.logical_not(low)
            keep, come = keep_ref[j, way], come_ref[j, way]
            out[way] = jnp.where(scaled, keep, come) * kept_ref[1 - way, j] + jnp.where(
                scaled, come, keep
            )


ORDERS = ((0, 1, 2, 3), (3, 2, 1, 0))


def totals_kernel(place_ref, r0, r1, r2, r3, d_ref, out_ref, sorted_ref):
    for turn, ref in enumerate((r0, r1, r2, r3)):
        sorted_ref[lax.rem(place_ref[1] - turn + CHIPS, CHIPS)] = ref[...]
    for way, order in enumerate(ORDERS):
        total = sorted_ref[order[0], way]
        for c in order[1:]:
            total = total * d_ref[c : c + 1, :] + sorted_ref[c, way]
        out_ref[16 * way : 16 * way + 16, :, :GC] = total.reshape(16, 8, GC)
    for tile in range(PAIRS):
        row = d_ref[CHIPS : CHIPS + 1, 128 * tile : 128 * tile + 128]
        out_ref[:, tile : tile + 1, GC:] = jnp.broadcast_to(row[None], (32, 1, 128))
    out_ref[:, PAIRS:, GC:] = jnp.zeros((32, 8 - PAIRS, 128), F32)


def chain_kernel(flag_ref, p_ref, out_ref):
    backward = flag_ref[0] == 1
    state = [jnp.zeros((8, 128), F32) for _ in range(PAIRS)]
    for s in range(32):
        k = jnp.where(backward, 31 - s, s)
        for t in range(PAIRS):
            columns = slice(128 * t, 128 * t + 128)
            out_ref[k, :, columns] = state[t]
            state[t] = state[t] * p_ref[k, t : t + 1, GC:] + p_ref[k, :, columns]


def entering_kernel(place_ref, sorted_ref, d_ref, edge_ref, o0, o1, o2, o3, all_ref):
    for way, order in enumerate(ORDERS):
        e = edge_ref[16 * way : 16 * way + 16].reshape(N, GC)
        for c in order:
            all_ref[c, way] = e
            if c != order[-1]:
                e = e * d_ref[c : c + 1, :] + sorted_ref[c, way]
    for turn, out in enumerate((o0, o1, o2, o3)):
        out[...] = all_ref[lax.rem(place_ref[1] + turn, CHIPS)].astype(RETURN)


def fork_kernel(place_ref, r0, r1, r2, r3, keep_ref, come_ref, kept_ref, mine_ref, send_ref):
    low = place_ref[0] == 0
    for turn, ref in enumerate((r0, r1, r2, r3)):
        j = lax.rem(place_ref[1] - turn + CHIPS, CHIPS)
        for way in range(2):
            direct_is_mine = low if way == 0 else jnp.logical_not(low)
            direct = ref[way].astype(F32)
            passed = jnp.where(direct_is_mine, keep_ref[j, way], come_ref[j, way])
            through = kept_ref[way, j] * direct + passed
            mine_ref[j, way] = jnp.where(direct_is_mine, direct, through)
            send_ref[j, way] = jnp.where(direct_is_mine, through, direct)


def finish_kernel(
    place, x_ref, dy_ref, cum_ref, cumt_ref, y_ref, dx_ref, mine_ref, come_ref, gain_ref, b_ref, c_ref,
    db0_ref, dc0_ref, out_ref, gs_ref, o0, o1, o2, o3, db_ref, dc_ref, gd_ref,
):
    step = pl.program_id(0)
    low_core = place[0] == 0

    @pl.when(step == 0)
    def _():
        db_ref[...] = db0_ref[...]
        dc_ref[...] = dc0_ref[...]

    def both(way):
        mine, come = mine_ref[0, way], come_ref[0, way]
        return jnp.concatenate([jnp.where(low_core, mine, come), jnp.where(low_core, come, mine)], axis=1)

    cums = cum_ref[0], cum_ref[1]
    from_start = jnp.concatenate([spread(jnp.exp(v)) for v in cums], axis=1)
    to_end = jnp.concatenate([spread(jnp.exp(v[ROWS - 1 : ROWS, :] - v)) for v in cums], axis=1)
    gain = jnp.concatenate([gain_ref[0], gain_ref[1]], axis=1)
    x = x_ref[...].astype(F32)
    dy = dy_ref[...].astype(F32)
    entering, leaving = both(0), both(1)
    b, c = b_ref[...], c_ref[...]

    def carried(matrix, state, scale, v):
        parts = jnp.concatenate(halves(state), axis=0)
        product = scale * dot(jnp.concatenate([matrix, matrix], axis=1), parts)
        high, low = halves(scale * v)
        wide = dot(high, parts, NT)
        return product, wide[:, :N] + wide[:, N:] + dot(low, parts[:N], NT)

    y_carried, dc = carried(c, entering, from_start, dy)
    dx_carried, db = carried(b, leaving, to_end, x)
    y = y_ref[...] + y_carried
    dx_in = dx_ref[...]
    out_ref[...] = (y + gain * x).astype(BF16)
    gs_ref[...] = (dx_in + dx_carried + gain * dy).astype(BF16)
    dc_ref[...] += dc
    db_ref[...] += db
    of_head = (
        lax.broadcasted_iota(jnp.int32, (32, 2 * GC), 1) // GC * 16
        + lax.broadcasted_iota(jnp.int32, (32, 2 * GC), 1) % GC // HEAD
        == lax.broadcasted_iota(jnp.int32, (32, 2 * GC), 0)
    ).astype(BF16)

    def by_head(v):
        high, low = halves(v)
        return dot(of_head, high, NT) + dot(of_head, low, NT)

    product = jnp.sum(entering * leaving, axis=0, keepdims=True)
    across = by_head(jnp.broadcast_to(product, (8, 2 * GC)))[:, 0:1]
    t = lax.broadcasted_iota(jnp.int32, (ROWS, ROWS), 0)
    s = lax.broadcasted_iota(jnp.int32, (ROWS, ROWS), 1)
    after = (t >= s).astype(BF16)
    before = (t < s).astype(BF16)
    gd = across * jnp.exp(cumt_ref[...].reshape(32, ROWS)[:, ROWS - 1 : ROWS])
    for part in thirds(by_head(dy * y - x * dx_in)):
        gd += dot(part, after)
    for part in thirds(by_head(x * dx_carried)):
        gd += dot(part, before)
    gd_ref[step] = gd

    @pl.when(step == CHIPS - 1)
    def _():
        for turn, out in enumerate((o0, o1, o2, o3)):
            out[0:ROWS, :] = db_ref[...]
            out[ROWS : 2 * ROWS, :] = dc_ref[...]
            mine = gd_ref[lax.rem(place[1] + turn, CHIPS)]
            out[384:416, :] = mine[:, 0:128]
            out[416:448, 0:64] = mine[:, 128:192]
            out[416:448, 64:128] = jnp.zeros((32, 64), F32)


def finish(place, x, dy, cum, cumt, y, dx, mine, come, gain, b, c, db, dc):
    columns = pl.BlockSpec((ROWS, 2 * GC), lambda s, place: (0, s))
    by_chip = lambda *shape: pl.BlockSpec((2, *shape), lambda s, place: (s, 0, 0))
    quad = pl.BlockSpec((1, *PAIR), lambda s, place: (s, 0, 0, 0))
    whole = lambda *shape: pl.BlockSpec(shape, lambda s, place: (0, 0))
    wide = jax.ShapeDtypeStruct((ROWS, GC * GROUPS), BF16)
    return pl.pallas_call(
        finish_kernel,
        grid_spec=pltpu.PrefetchScalarGridSpec(
            num_scalar_prefetch=1,
            grid=(CHIPS,),
            in_specs=[
                columns, columns, by_chip(ROWS, 16), by_chip(16, ROWS), columns, columns, quad, quad,
                by_chip(1, GC), *[whole(ROWS, N)] * 4,
            ],
            out_specs=[columns, columns] + [whole(448, 128)] * 4,
            scratch_shapes=[
                pltpu.VMEM((ROWS, N), F32), pltpu.VMEM((ROWS, N), F32), pltpu.VMEM((CHIPS, 32, ROWS), F32),
            ],
        ),
        out_shape=[wide, wide] + [jax.ShapeDtypeStruct((448, 128), F32)] * 4,
        compiler_params=pltpu.CompilerParams(vmem_limit_bytes=60 << 20),
        name="finish",
    )(place, x, dy, cum, cumt, y, dx, mine, come, gain, b, c, db, dc)


def tie(*values):
    return lax.optimization_barrier(values)


def turned(v):
    r = {
        turn: lax.ppermute(v[turn], "y", [(i, (i + turn) % CHIPS) for i in range(CHIPS)])
        for turn in (2, 1, 3)
    }
    return [v[0], r[1], r[2], r[3]]


def gathered(parts, iy, low):
    by_chip = jnp.roll(jnp.stack([parts[0], parts[3], parts[2], parts[1]]), iy, axis=0)
    other = lax.ppermute(by_chip, "core", SWAP)
    return jnp.stack(
        [jnp.where(low, by_chip, other), jnp.where(low, other, by_chip)], axis=1
    ).reshape(GROUPS, *by_chip.shape[1:])


def shards(x, dy, b_all, c_all, log_decay, skip_gain):
    ix = lax.axis_index("x")
    iy, core = lax.axis_index("y"), lax.axis_index("core")
    place = jnp.stack([core, iy]).astype(jnp.int32)
    row0 = (2 * iy + core) * ROWS
    b = lax.dynamic_slice_in_dim(b_all, row0, ROWS, 0)
    c = lax.dynamic_slice_in_dim(c_all, row0, ROWS, 0)
    swap = lambda v: lax.ppermute(v, "core", SWAP)
    over_ctx = lambda v: lax.all_to_all(v, ("x", "z"), split_axis=0, concat_axis=0, tiled=True)
    pair = lambda dtype: jax.ShapeDtypeStruct(PAIR, dtype)
    quad = jax.ShapeDtypeStruct((CHIPS, *PAIR), F32)

    ldt = log_decay.T
    [packed] = on_chip(
        pack_kernel, "pack", [jax.ShapeDtypeStruct((GROUPS, 2, 16, ROWS), F32)],
        ldt, skip_gain.reshape(1, HG), scalars=0,
    )
    got = lax.all_to_all(packed, ("y", "core"), split_axis=0, concat_axis=0, tiled=True)
    cumt, cum, gain, kept = on_chip(
        decays_kernel, "decays",
        [
            jax.ShapeDtypeStruct((GROUPS, 16, ROWS), F32),
            jax.ShapeDtypeStruct((GROUPS, ROWS, 16), F32),
            jax.ShapeDtypeStruct((GROUPS, 1, GC), F32),
            jax.ShapeDtypeStruct((2, CHIPS, 1, GC), F32),
        ],
        place, got,
    )
    send, keep = chunk_states(place, x, dy, cum, b.T, c.T)
    come = swap(send)
    out = on_chip(join_kernel, "join", [pair(F32)] * 4, place, keep, come, kept)
    parts = turned(out)
    x_w, dy_w, ldt_w, _ = tie(x, dy, ldt, out[0])
    [own] = on_chip(owner_kernel, "owner_decays", [jax.ShapeDtypeStruct((8, GC), F32)], ldt_w, scalars=0)
    inside = within(x_w, dy_w, cum, cumt, b, c)
    y_in, dx_in, db_in, dc_in, *parts = tie(*inside, *parts)
    total, by_chip = on_chip(
        totals_kernel, "totals", [jax.ShapeDtypeStruct((32, 8, GC + 128), F32), quad], place, *parts, own
    )
    total = over_ctx(total)
    flag = (ix >= 2).reshape(1).astype(jnp.int32)
    [edge] = on_chip(
        chain_kernel, "chain", [jax.ShapeDtypeStruct((32, 8, GC), F32)], flag, total
    )
    edge = over_ctx(edge)
    out = on_chip(
        entering_kernel, "entering", [pair(RETURN)] * 4, place, by_chip, own, edge,
        scratch=[pltpu.VMEM((CHIPS, *PAIR), F32)],
    )
    mine, send = on_chip(fork_kernel, "fork", [quad] * 2, place, *turned(out), keep, come, kept)
    scan_out, grad_x, *ends = finish(
        place, x, dy, cum, cumt, y_in, dx_in, mine, swap(send), gain, b, c, db_in, dc_in
    )
    ends = gathered(turned(ends), iy, core == 0)
    grad_b = ends[:, :ROWS].reshape(GROUPS * ROWS, N)
    grad_c = ends[:, ROWS : 2 * ROWS].reshape(GROUPS * ROWS, N)
    rest = ends[:, 2 * ROWS :].reshape(GROUPS, 2, 2, 16, 128)
    rest = lax.dynamic_index_in_dim(rest, core, 2, keepdims=False)
    rest = jnp.concatenate([rest[:, 0, :HG], rest[:, 1, :HG, :64]], axis=2)
    grad_decay = rest.transpose(0, 2, 1).reshape(GROUPS * ROWS, HG)
    return scan_out, grad_x, grad_b, grad_c, grad_decay


def solution(mesh):
    grid = Mesh(mesh.devices.reshape(4, 8, 4, 2), ("x", "z", "y", "core"))
    ctx, head = ("x", "z"), ("y", "core")
    rows = P((*ctx, *head), None)
    return jax.shard_map(
        shards,
        mesh=grid,
        in_specs=(rows, rows, P(ctx, None), P(ctx, None), P(ctx, head), P(head)),
        out_specs=(rows, rows, P(ctx, None), P(ctx, None), P(ctx, head)),
        check_vma=False,
    )
```

```python
import functools

import jax
import jax.numpy as jnp
from jax import lax
from jax.experimental import pallas as pl
from jax.experimental.pallas import tpu as pltpu
from jax.sharding import Mesh
from jax.sharding import PartitionSpec as P

ROWS = 192
N = 128
HEAD = 64
HG = 10
GC = HG * HEAD
GROUPS = 8
PAIRS = GC // 128
F32, BF16 = jnp.float32, jnp.bfloat16
SWAP = [(0, 1), (1, 0)]
NN = (((1,), (0,)), ((), ()))
NT = (((1,), (1,)), ((), ()))
TN = (((0,), (0,)), ((), ()))


def dot(a, b, dims=NN):
    return lax.dot_general(a, b, dims, preferred_element_type=F32)


def halves(v):
    high = v.astype(BF16)
    return high, (v - high.astype(F32)).astype(BF16)


def thirds(v):
    high = v.astype(BF16)
    rest = v - high.astype(F32)
    middle = rest.astype(BF16)
    return high, middle, (rest - middle.astype(F32)).astype(BF16)


def spread(columns):
    rows = columns.shape[0]
    first = lax.broadcasted_iota(jnp.int32, (rows, 128), 1) < HEAD
    return jnp.concatenate(
        [
            jnp.where(
                first,
                jnp.broadcast_to(columns[:, 2 * p : 2 * p + 1], (rows, 128)),
                jnp.broadcast_to(columns[:, 2 * p + 1 : 2 * p + 2], (rows, 128)),
            )
            for p in range(PAIRS)
        ],
        axis=1,
    )


def within_kernel(
    x_ref, dy_ref, cum_ref, cumt_ref, b_ref, c_ref, y_ref, dx_ref, db_ref, dc_ref, score_ref, acc_ref
):
    step = pl.program_id(0)
    causal = lax.broadcasted_iota(jnp.int32, (ROWS, ROWS), 0) >= lax.broadcasted_iota(
        jnp.int32, (ROWS, ROWS), 1
    )

    @pl.when(step == 0)
    def _():
        score_ref[...] = jnp.where(causal, dot(c_ref[...], b_ref[...], NT), 0.0)
        acc_ref[...] = jnp.zeros_like(acc_ref)

    first = lax.broadcasted_iota(jnp.int32, (ROWS, 128), 1) < HEAD
    zero = jnp.zeros((ROWS, 128), BF16)
    for p in range(PAIRS):
        columns = slice(128 * p, 128 * p + 128)
        x = x_ref[:, columns]
        dy = dy_ref[:, columns]
        y = dx = None
        for side in range(2):
            h = 2 * p + side
            keep = first if side == 0 else jnp.logical_not(first)
            xs = jnp.where(keep, x, zero)
            dys = jnp.where(keep, dy, zero)
            decay = jnp.exp(
                jnp.minimum(cum_ref[0, :, h : h + 1] - cumt_ref[0, h : h + 1, :], 0.0)
            )
            weights = (score_ref[...] * decay).astype(BF16)
            part = dot(weights, xs)
            y = part if y is None else y + part
            dweights = dot(dys, x, NT).astype(BF16).astype(F32)
            acc_ref[...] += dweights * decay
            part = dot(weights, dys, TN)
            dx = part if dx is None else dx + part
        y_ref[:, columns] = y
        dx_ref[:, columns] = dx

    @pl.when(step == GROUPS - 1)
    def _():
        high, low = halves(jnp.where(causal, acc_ref[...], 0.0))
        b, c = b_ref[...], c_ref[...]
        dc_ref[...] = dot(high, b) + dot(low, b)
        db_ref[...] = dot(high, c, TN) + dot(low, c, TN)


def within(x, dy, cum, cumt, b, c):
    by_column = pl.BlockSpec((ROWS, GC), lambda s: (0, s))
    whole = pl.BlockSpec((ROWS, N), lambda s: (0, 0))
    wide = jax.ShapeDtypeStruct((ROWS, GC * GROUPS), F32)
    small = jax.ShapeDtypeStruct((ROWS, N), F32)
    return pl.pallas_call(
        within_kernel,
        grid=(GROUPS,),
        in_specs=[
            by_column,
            by_column,
            pl.BlockSpec((1, ROWS, 16), lambda s: (s, 0, 0)),
            pl.BlockSpec((1, 16, ROWS), lambda s: (s, 0, 0)),
            whole,
            whole,
        ],
        out_specs=[by_column, by_column, whole, whole],
        out_shape=[wide, wide, small, small],
        scratch_shapes=[pltpu.VMEM((ROWS, ROWS), F32), pltpu.VMEM((ROWS, ROWS), F32)],
        compiler_params=pltpu.CompilerParams(vmem_limit_bytes=40 << 20),
        cost_estimate=pl.CostEstimate(
            flops=20_000_000_000, bytes_accessed=12_000_000, transcendentals=3_000_000
        ),
        name="within_chunk",
    )(x, dy, cum, cumt, b, c)


CHIPS = 4
VMEM = pl.BlockSpec(memory_space=pltpu.VMEM)
SMEM = pl.BlockSpec(memory_space=pltpu.SMEM)
PAIR = (2, N, GC)
LOWS = 64


def on_chip(kernel, name, outs, *args, scratch=(), scalars=1):
    return pl.pallas_call(
        kernel,
        in_specs=[SMEM] * scalars + [VMEM] * (len(args) - scalars),
        out_specs=[VMEM] * len(outs),
        out_shape=outs,
        scratch_shapes=list(scratch),
        compiler_params=pltpu.CompilerParams(vmem_limit_bytes=44 << 20),
        name=name,
    )(*args)


def pack_kernel(ld_ref, gain_ref, out_ref):
    out_ref[...] = jnp.zeros_like(out_ref)
    for chunk in range(GROUPS):
        rows = ld_ref[:, chunk * ROWS : (chunk + 1) * ROWS]
        for core in range(2):
            at = 2 * (chunk // 2) + core
            out_ref[at, chunk % 2, 0:HG, :] = rows
            out_ref[at, chunk % 2, HG : HG + 1, 0:HG] = gain_ref[...]


def owner_kernel(ld_ref, out_ref):
    width = 2 * ROWS
    of = lax.broadcasted_iota(jnp.int32, (8, 8 * ROWS), 1) // width
    row = lax.broadcasted_iota(jnp.int32, (8, 8 * ROWS), 0)
    pick = jnp.logical_or(of == row, row == CHIPS).astype(BF16)
    totals = sum(dot(pick, part, NT) for part in thirds(ld_ref[...]))
    out_ref[...] = spread(jnp.exp(totals))


def decays_kernel(core_ref, got_ref, cumt_ref, cum_ref, gain_ref, kept_ref):
    low = core_ref[0] == 0
    t = lax.broadcasted_iota(jnp.int32, (ROWS, ROWS), 0)
    s = lax.broadcasted_iota(jnp.int32, (ROWS, ROWS), 1)
    upper = (t <= s).astype(BF16)
    lower = (t >= s).astype(BF16)
    is_head = lax.broadcasted_iota(jnp.int32, (GROUPS, 16, ROWS), 1) < HG
    flat, tall = [], []
    for half in range(2):
        ld = jnp.where(is_head, got_ref[:, half], 0.0).reshape(GROUPS * 16, ROWS)
        parts = thirds(ld)
        flat.append(sum(dot(part, upper) for part in parts))
        tall.append(sum(dot(lower, part, NT) for part in parts))
    cumt_ref[...] = jnp.where(low, flat[0], flat[1]).reshape(GROUPS, 16, ROWS)
    own = jnp.where(low, tall[0], tall[1])
    for g in range(GROUPS):
        cum_ref[g] = own[:, 16 * g : 16 * g + 16]
        gain_ref[g] = spread(got_ref[g, 0, HG : HG + 1, :])
    for half in range(2):
        ends = jnp.exp(tall[half][ROWS - 1 : ROWS, :])
        for j in range(CHIPS):
            a = ends[:, 32 * j : 32 * j + 16]
            b = ends[:, 32 * j + 16 : 32 * j + 32]
            kept_ref[half, j] = spread(jnp.where(low, a, b))


def states_kernel(place, x_ref, dy_ref, cum_ref, bt_ref, ct_ref, send_ref, keep_ref):
    low = place[0] == 0
    for way, (v_ref, m_ref) in enumerate(((x_ref, bt_ref), (dy_ref, ct_ref))):
        m = m_ref[...]
        states = []
        for k in range(2):
            cum = cum_ref[k]
            scale = jnp.exp(cum[ROWS - 1 : ROWS, :] - cum if way == 0 else cum)
            high, low_part = halves(v_ref[:, k * GC : (k + 1) * GC].astype(F32) * spread(scale))
            states.append(dot(m, high) + dot(m, low_part))
        keep_ref[0, way] = jnp.where(low, states[0], states[1])
        send_ref[0, way] = jnp.where(low, states[1], states[0])


def chunk_states(place, x, dy, cum, bt, ct):
    columns = pl.BlockSpec((ROWS, 2 * GC), lambda s, place: (0, s))
    whole = pl.BlockSpec((N, ROWS), lambda s, place: (0, 0))
    quad = pl.BlockSpec((1, *PAIR), lambda s, place: (s, 0, 0, 0))
    return pl.pallas_call(
        states_kernel,
        grid_spec=pltpu.PrefetchScalarGridSpec(
            num_scalar_prefetch=1,
            grid=(CHIPS,),
            in_specs=[
                columns,
                columns,
                pl.BlockSpec((2, ROWS, 16), lambda s, place: (s, 0, 0)),
                whole,
                whole,
            ],
            out_specs=[quad, quad],
        ),
        out_shape=[jax.ShapeDtypeStruct((CHIPS, *PAIR), F32)] * 2,
        compiler_params=pltpu.CompilerParams(vmem_limit_bytes=60 << 20),
        name="chunk_states",
    )(place, x, dy, cum, bt, ct)


def join_kernel(place_ref, keep_ref, come_ref, kept_ref, *outs):
    low = place_ref[0] == 0
    for turn, out in enumerate(outs):
        j = lax.rem(place_ref[1] + turn, CHIPS)
        for way in range(2):
            scaled = low if way == 0 else jnp.logical_not(low)
            keep, come = keep_ref[j, way], come_ref[j, way]
            out[way] = jnp.where(scaled, keep, come) * kept_ref[1 - way, j] + jnp.where(
                scaled, come, keep
            )


ORDERS = ((0, 1, 2, 3), (3, 2, 1, 0))


def totals_kernel(place_ref, r0, r1, r2, r3, d_ref, out_ref, sorted_ref):
    for turn, ref in enumerate((r0, r1, r2, r3)):
        sorted_ref[lax.rem(place_ref[1] - turn + CHIPS, CHIPS)] = ref[...]
    for way, order in enumerate(ORDERS):
        total = sorted_ref[order[0], way]
        for c in order[1:]:
            total = total * d_ref[c : c + 1, :] + sorted_ref[c, way]
        out_ref[16 * way : 16 * way + 16, :, :GC] = total.reshape(16, 8, GC)
    for tile in range(PAIRS):
        row = d_ref[CHIPS : CHIPS + 1, 128 * tile : 128 * tile + 128]
        out_ref[:, tile : tile + 1, GC:] = jnp.broadcast_to(row[None], (32, 1, 128))
    out_ref[:, PAIRS:, GC:] = jnp.zeros((32, 8 - PAIRS, 128), F32)


def chain_kernel(flag_ref, p_ref, out_ref):
    backward = flag_ref[0] == 1
    state = [jnp.zeros((8, 128), F32) for _ in range(PAIRS)]
    for s in range(32):
        k = jnp.where(backward, 31 - s, s)
        for t in range(PAIRS):
            columns = slice(128 * t, 128 * t + 128)
            out_ref[k, :, columns] = state[t]
            state[t] = state[t] * p_ref[k, t : t + 1, GC:] + p_ref[k, :, columns]


def entering_kernel(place_ref, sorted_ref, d_ref, edge_ref, o0, o1, o2, o3, all_ref):
    for way, order in enumerate(ORDERS):
        e = edge_ref[16 * way : 16 * way + 16].reshape(N, GC)
        for c in order:
            all_ref[c, way] = e
            if c != order[-1]:
                e = e * d_ref[c : c + 1, :] + sorted_ref[c, way]
    for turn, out in enumerate((o0, o1, o2, o3)):
        at = lax.rem(place_ref[1] + turn, CHIPS)
        for way in range(2):
            high, low = halves(all_ref[at, way])
            out[way, :N] = high
            out[way, N:] = low[:LOWS]


def fork_kernel(place_ref, r0, r1, r2, r3, keep_ref, come_ref, kept_ref, mine_ref, send_ref):
    low = place_ref[0] == 0
    for turn, ref in enumerate((r0, r1, r2, r3)):
        j = lax.rem(place_ref[1] - turn + CHIPS, CHIPS)
        for way in range(2):
            direct_is_mine = low if way == 0 else jnp.logical_not(low)
            low_rows = jnp.concatenate(
                [ref[way, N:].astype(F32), jnp.zeros((N - LOWS, GC), F32)], axis=0
            )
            direct = ref[way, :N].astype(F32) + low_rows
            passed = jnp.where(direct_is_mine, keep_ref[j, way], come_ref[j, way])
            through = kept_ref[way, j] * direct + passed
            mine_ref[j, way] = jnp.where(direct_is_mine, direct, through)
            send_ref[j, way] = jnp.where(direct_is_mine, through, direct)


def finish_kernel(
    place, x_ref, dy_ref, cum_ref, cumt_ref, y_ref, dx_ref, mine_ref, come_ref, gain_ref, b_ref, c_ref,
    db0_ref, dc0_ref, out_ref, gs_ref, o0, o1, o2, o3, db_ref, dc_ref, gd_ref,
):
    step = pl.program_id(0)
    low_core = place[0] == 0

    @pl.when(step == 0)
    def _():
        db_ref[...] = db0_ref[...]
        dc_ref[...] = dc0_ref[...]

    def both(way):
        mine, come = mine_ref[0, way], come_ref[0, way]
        return jnp.concatenate([jnp.where(low_core, mine, come), jnp.where(low_core, come, mine)], axis=1)

    cums = cum_ref[0], cum_ref[1]
    from_start = jnp.concatenate([spread(jnp.exp(v)) for v in cums], axis=1)
    to_end = jnp.concatenate([spread(jnp.exp(v[ROWS - 1 : ROWS, :] - v)) for v in cums], axis=1)
    gain = jnp.concatenate([gain_ref[0], gain_ref[1]], axis=1)
    x = x_ref[...].astype(F32)
    dy = dy_ref[...].astype(F32)
    entering, leaving = both(0), both(1)
    b, c = b_ref[...], c_ref[...]

    def carried(matrix, state, scale, v):
        parts = jnp.concatenate(halves(state), axis=0)
        product = scale * dot(jnp.concatenate([matrix, matrix], axis=1), parts)
        high, low = halves(scale * v)
        wide = dot(high, parts, NT)
        return product, wide[:, :N] + wide[:, N:] + dot(low, parts[:N], NT)

    y_carried, dc = carried(c, entering, from_start, dy)
    dx_carried, db = carried(b, leaving, to_end, x)
    y = y_ref[...] + y_carried
    dx_in = dx_ref[...]
    out_ref[...] = (y + gain * x).astype(BF16)
    gs_ref[...] = (dx_in + dx_carried + gain * dy).astype(BF16)
    dc_ref[...] += dc
    db_ref[...] += db
    of_head = (
        lax.broadcasted_iota(jnp.int32, (32, 2 * GC), 1) // GC * 16
        + lax.broadcasted_iota(jnp.int32, (32, 2 * GC), 1) % GC // HEAD
        == lax.broadcasted_iota(jnp.int32, (32, 2 * GC), 0)
    ).astype(BF16)

    def by_head(v):
        high, low = halves(v)
        return dot(of_head, high, NT) + dot(of_head, low, NT)

    x_dx = x * dx_carried
    row = from_start[ROWS - 1 : ROWS, :] * jnp.sum(entering * leaving, axis=0, keepdims=True)
    row += jnp.sum(x_dx, axis=0, keepdims=True)
    t = lax.broadcasted_iota(jnp.int32, (ROWS, ROWS), 0)
    s = lax.broadcasted_iota(jnp.int32, (ROWS, ROWS), 1)
    after = (t >= s).astype(BF16)
    gd = jnp.broadcast_to(by_head(jnp.broadcast_to(row, (8, 2 * GC)))[:, 0:1], (32, ROWS))
    for part in thirds(by_head(dy * y - (x * dx_in + x_dx))):
        gd += dot(part, after)
    gd_ref[step] = gd

    @pl.when(step == CHIPS - 1)
    def _():
        for turn, out in enumerate((o0, o1, o2, o3)):
            out[0:ROWS, :] = db_ref[...]
            out[ROWS : 2 * ROWS, :] = dc_ref[...]
            mine = gd_ref[lax.rem(place[1] + turn, CHIPS)]
            out[384:416, :] = mine[:, 0:128]
            out[416:448, 0:64] = mine[:, 128:192]
            out[416:448, 64:128] = jnp.zeros((32, 64), F32)


def finish(place, x, dy, cum, cumt, y, dx, mine, come, gain, b, c, db, dc):
    columns = pl.BlockSpec((ROWS, 2 * GC), lambda s, place: (0, s))
    by_chip = lambda *shape: pl.BlockSpec((2, *shape), lambda s, place: (s, 0, 0))
    quad = pl.BlockSpec((1, *PAIR), lambda s, place: (s, 0, 0, 0))
    whole = lambda *shape: pl.BlockSpec(shape, lambda s, place: (0, 0))
    wide = jax.ShapeDtypeStruct((ROWS, GC * GROUPS), BF16)
    return pl.pallas_call(
        finish_kernel,
        grid_spec=pltpu.PrefetchScalarGridSpec(
            num_scalar_prefetch=1,
            grid=(CHIPS,),
            in_specs=[
                columns, columns, by_chip(ROWS, 16), by_chip(16, ROWS), columns, columns, quad, quad,
                by_chip(1, GC), *[whole(ROWS, N)] * 4,
            ],
            out_specs=[columns, columns] + [whole(448, 128)] * 4,
            scratch_shapes=[
                pltpu.VMEM((ROWS, N), F32), pltpu.VMEM((ROWS, N), F32), pltpu.VMEM((CHIPS, 32, ROWS), F32),
            ],
        ),
        out_shape=[wide, wide] + [jax.ShapeDtypeStruct((448, 128), F32)] * 4,
        compiler_params=pltpu.CompilerParams(vmem_limit_bytes=60 << 20),
        name="finish",
    )(place, x, dy, cum, cumt, y, dx, mine, come, gain, b, c, db, dc)


def tie(*values):
    return lax.optimization_barrier(values)


def turned(v):
    r = {
        turn: lax.ppermute(v[turn], "y", [(i, (i + turn) % CHIPS) for i in range(CHIPS)])
        for turn in (2, 1, 3)
    }
    return [v[0], r[1], r[2], r[3]]


def gathered(parts, iy, low):
    by_chip = jnp.roll(jnp.stack([parts[0], parts[3], parts[2], parts[1]]), iy, axis=0)
    other = lax.ppermute(by_chip, "core", SWAP)
    return jnp.stack(
        [jnp.where(low, by_chip, other), jnp.where(low, other, by_chip)], axis=1
    ).reshape(GROUPS, *by_chip.shape[1:])


def shards(x, dy, b_all, c_all, log_decay, skip_gain):
    ix = lax.axis_index("x")
    iy, core = lax.axis_index("y"), lax.axis_index("core")
    place = jnp.stack([core, iy]).astype(jnp.int32)
    row0 = (2 * iy + core) * ROWS
    b = lax.dynamic_slice_in_dim(b_all, row0, ROWS, 0)
    c = lax.dynamic_slice_in_dim(c_all, row0, ROWS, 0)
    swap = lambda v: lax.ppermute(v, "core", SWAP)
    over_ctx = lambda v: lax.all_to_all(v, ("x", "z"), split_axis=0, concat_axis=0, tiled=True)
    pair = lambda dtype: jax.ShapeDtypeStruct(PAIR, dtype)
    quad = jax.ShapeDtypeStruct((CHIPS, *PAIR), F32)

    ldt = log_decay.T
    [packed] = on_chip(
        pack_kernel, "pack", [jax.ShapeDtypeStruct((GROUPS, 2, 16, ROWS), F32)],
        ldt, skip_gain.reshape(1, HG), scalars=0,
    )
    got = lax.all_to_all(packed, ("y", "core"), split_axis=0, concat_axis=0, tiled=True)
    cumt, cum, gain, kept = on_chip(
        decays_kernel, "decays",
        [
            jax.ShapeDtypeStruct((GROUPS, 16, ROWS), F32),
            jax.ShapeDtypeStruct((GROUPS, ROWS, 16), F32),
            jax.ShapeDtypeStruct((GROUPS, 1, GC), F32),
            jax.ShapeDtypeStruct((2, CHIPS, 1, GC), F32),
        ],
        place, got,
    )
    send, keep = chunk_states(place, x, dy, cum, b.T, c.T)
    come = swap(send)
    out = on_chip(join_kernel, "join", [pair(F32)] * 4, place, keep, come, kept)
    parts = turned(out)
    x_w, dy_w, ldt_w, _ = tie(x, dy, ldt, out[0])
    [own] = on_chip(owner_kernel, "owner_decays", [jax.ShapeDtypeStruct((8, GC), F32)], ldt_w, scalars=0)
    inside = within(x_w, dy_w, cum, cumt, b, c)
    y_in, dx_in, db_in, dc_in, *parts = tie(*inside, *parts)
    total, by_chip = on_chip(
        totals_kernel, "totals", [jax.ShapeDtypeStruct((32, 8, GC + 128), F32), quad], place, *parts, own
    )
    total = over_ctx(total)
    flag = (ix >= 2).reshape(1).astype(jnp.int32)
    [edge] = on_chip(
        chain_kernel, "chain", [jax.ShapeDtypeStruct((32, 8, GC), F32)], flag, total
    )
    edge = over_ctx(edge)
    out = on_chip(
        entering_kernel, "entering", [jax.ShapeDtypeStruct((2, N + LOWS, GC), BF16)] * 4, place, by_chip, own, edge,
        scratch=[pltpu.VMEM((CHIPS, *PAIR), F32)],
    )
    mine, send = on_chip(fork_kernel, "fork", [quad] * 2, place, *turned(out), keep, come, kept)
    scan_out, grad_x, *ends = finish(
        place, x, dy, cum, cumt, y_in, dx_in, mine, swap(send), gain, b, c, db_in, dc_in
    )
    ends = gathered(turned(ends), iy, core == 0)
    grad_b = ends[:, :ROWS].reshape(GROUPS * ROWS, N)
    grad_c = ends[:, ROWS : 2 * ROWS].reshape(GROUPS * ROWS, N)
    rest = ends[:, 2 * ROWS :].reshape(GROUPS, 2, 2, 16, 128)
    rest = lax.dynamic_index_in_dim(rest, core, 2, keepdims=False)
    rest = jnp.concatenate([rest[:, 0, :HG], rest[:, 1, :HG, :64]], axis=2)
    grad_decay = rest.transpose(0, 2, 1).reshape(GROUPS * ROWS, HG)
    return scan_out, grad_x, grad_b, grad_c, grad_decay


def solution(mesh):
    grid = Mesh(mesh.devices.reshape(4, 8, 4, 2), ("x", "z", "y", "core"))
    ctx, head = ("x", "z"), ("y", "core")
    rows = P((*ctx, *head), None)
    return jax.shard_map(
        shards,
        mesh=grid,
        in_specs=(rows, rows, P(ctx, None), P(ctx, None), P(ctx, head), P(head)),
        out_specs=(rows, rows, P(ctx, None), P(ctx, None), P(ctx, head)),
        check_vma=False,
    )
```

```python
import functools

import jax
import jax.numpy as jnp
from jax import lax
from jax.experimental import pallas as pl
from jax.experimental.pallas import tpu as pltpu
from jax.sharding import Mesh
from jax.sharding import PartitionSpec as P

ROWS = 192
N = 128
HEAD = 64
HG = 10
GC = HG * HEAD
GROUPS = 8
PAIRS = GC // 128
F32, BF16 = jnp.float32, jnp.bfloat16
SWAP = [(0, 1), (1, 0)]
NN = (((1,), (0,)), ((), ()))
NT = (((1,), (1,)), ((), ()))
TN = (((0,), (0,)), ((), ()))


def dot(a, b, dims=NN):
    return lax.dot_general(a, b, dims, preferred_element_type=F32)


def halves(v):
    high = v.astype(BF16)
    return high, (v - high.astype(F32)).astype(BF16)


def thirds(v):
    high = v.astype(BF16)
    rest = v - high.astype(F32)
    middle = rest.astype(BF16)
    return high, middle, (rest - middle.astype(F32)).astype(BF16)


def spread(columns):
    rows = columns.shape[0]
    first = lax.broadcasted_iota(jnp.int32, (rows, 128), 1) < HEAD
    return jnp.concatenate(
        [
            jnp.where(
                first,
                jnp.broadcast_to(columns[:, 2 * p : 2 * p + 1], (rows, 128)),
                jnp.broadcast_to(columns[:, 2 * p + 1 : 2 * p + 2], (rows, 128)),
            )
            for p in range(PAIRS)
        ],
        axis=1,
    )


def within_kernel(
    x_ref, dy_ref, cum_ref, cumt_ref, b_ref, c_ref, y_ref, dx_ref, db_ref, dc_ref, score_ref, acc_ref
):
    step = pl.program_id(0)
    causal = lax.broadcasted_iota(jnp.int32, (ROWS, ROWS), 0) >= lax.broadcasted_iota(
        jnp.int32, (ROWS, ROWS), 1
    )

    @pl.when(step == 0)
    def _():
        score_ref[...] = jnp.where(causal, dot(c_ref[...], b_ref[...], NT), 0.0)
        acc_ref[...] = jnp.zeros_like(acc_ref)

    first = lax.broadcasted_iota(jnp.int32, (ROWS, 128), 1) < HEAD
    zero = jnp.zeros((ROWS, 128), BF16)
    for p in range(PAIRS):
        columns = slice(128 * p, 128 * p + 128)
        x = x_ref[:, columns]
        dy = dy_ref[:, columns]
        y = dx = None
        for side in range(2):
            h = 2 * p + side
            keep = first if side == 0 else jnp.logical_not(first)
            xs = jnp.where(keep, x, zero)
            dys = jnp.where(keep, dy, zero)
            decay = jnp.exp(
                jnp.minimum(cum_ref[0, :, h : h + 1] - cumt_ref[0, h : h + 1, :], 0.0)
            )
            weights = (score_ref[...] * decay).astype(BF16)
            part = dot(weights, xs)
            y = part if y is None else y + part
            dweights = dot(dys, x, NT).astype(BF16).astype(F32)
            acc_ref[...] += dweights * decay
            part = dot(weights, dys, TN)
            dx = part if dx is None else dx + part
        y_ref[:, columns] = y
        dx_ref[:, columns] = dx

    @pl.when(step == GROUPS - 1)
    def _():
        high, low = halves(jnp.where(causal, acc_ref[...], 0.0))
        b, c = b_ref[...], c_ref[...]
        dc_ref[...] = dot(high, b) + dot(low, b)
        db_ref[...] = dot(high, c, TN) + dot(low, c, TN)


def within(x, dy, cum, cumt, b, c):
    by_column = pl.BlockSpec((ROWS, GC), lambda s: (0, s))
    whole = pl.BlockSpec((ROWS, N), lambda s: (0, 0))
    wide = jax.ShapeDtypeStruct((ROWS, GC * GROUPS), F32)
    small = jax.ShapeDtypeStruct((ROWS, N), F32)
    return pl.pallas_call(
        within_kernel,
        grid=(GROUPS,),
        in_specs=[
            by_column,
            by_column,
            pl.BlockSpec((1, ROWS, 16), lambda s: (s, 0, 0)),
            pl.BlockSpec((1, 16, ROWS), lambda s: (s, 0, 0)),
            whole,
            whole,
        ],
        out_specs=[by_column, by_column, whole, whole],
        out_shape=[wide, wide, small, small],
        scratch_shapes=[pltpu.VMEM((ROWS, ROWS), F32), pltpu.VMEM((ROWS, ROWS), F32)],
        compiler_params=pltpu.CompilerParams(vmem_limit_bytes=40 << 20),
        cost_estimate=pl.CostEstimate(
            flops=20_000_000_000, bytes_accessed=12_000_000, transcendentals=3_000_000
        ),
        name="within_chunk",
    )(x, dy, cum, cumt, b, c)


CHIPS = 4
VMEM = pl.BlockSpec(memory_space=pltpu.VMEM)
SMEM = pl.BlockSpec(memory_space=pltpu.SMEM)
PAIR = (2, N, GC)
LOWS = 64


def on_chip(kernel, name, outs, *args, scratch=(), scalars=1):
    return pl.pallas_call(
        kernel,
        in_specs=[SMEM] * scalars + [VMEM] * (len(args) - scalars),
        out_specs=[VMEM] * len(outs),
        out_shape=outs,
        scratch_shapes=list(scratch),
        compiler_params=pltpu.CompilerParams(vmem_limit_bytes=44 << 20),
        name=name,
    )(*args)


def pack_kernel(ld_ref, gain_ref, out_ref):
    out_ref[...] = jnp.zeros_like(out_ref)
    for chunk in range(GROUPS):
        rows = ld_ref[:, chunk * ROWS : (chunk + 1) * ROWS]
        for core in range(2):
            at = 2 * (chunk // 2) + core
            out_ref[at, chunk % 2, 0:HG, :] = rows
            out_ref[at, chunk % 2, HG : HG + 1, 0:HG] = gain_ref[...]


def owner_kernel(ld_ref, out_ref):
    width = 2 * ROWS
    of = lax.broadcasted_iota(jnp.int32, (8, 8 * ROWS), 1) // width
    row = lax.broadcasted_iota(jnp.int32, (8, 8 * ROWS), 0)
    pick = jnp.logical_or(of == row, row == CHIPS).astype(BF16)
    totals = sum(dot(pick, part, NT) for part in thirds(ld_ref[...]))
    out_ref[...] = spread(jnp.exp(totals))


def decays_kernel(core_ref, got_ref, cumt_ref, cum_ref, gain_ref, kept_ref):
    low = core_ref[0] == 0
    t = lax.broadcasted_iota(jnp.int32, (ROWS, ROWS), 0)
    s = lax.broadcasted_iota(jnp.int32, (ROWS, ROWS), 1)
    upper = (t <= s).astype(BF16)
    lower = (t >= s).astype(BF16)
    is_head = lax.broadcasted_iota(jnp.int32, (GROUPS, 16, ROWS), 1) < HG
    flat, tall = [], []
    for half in range(2):
        ld = jnp.where(is_head, got_ref[:, half], 0.0).reshape(GROUPS * 16, ROWS)
        parts = thirds(ld)
        flat.append(sum(dot(part, upper) for part in parts))
        tall.append(sum(dot(lower, part, NT) for part in parts))
    cumt_ref[...] = jnp.where(low, flat[0], flat[1]).reshape(GROUPS, 16, ROWS)
    own = jnp.where(low, tall[0], tall[1])
    for g in range(GROUPS):
        cum_ref[g] = own[:, 16 * g : 16 * g + 16]
        gain_ref[g] = spread(got_ref[g, 0, HG : HG + 1, :])
    for half in range(2):
        ends = jnp.exp(tall[half][ROWS - 1 : ROWS, :])
        for j in range(CHIPS):
            a = ends[:, 32 * j : 32 * j + 16]
            b = ends[:, 32 * j + 16 : 32 * j + 32]
            kept_ref[half, j] = spread(jnp.where(low, a, b))


def states_kernel(place, x_ref, dy_ref, cum_ref, bt_ref, ct_ref, send_ref, keep_ref):
    low = place[0] == 0
    for way, (v_ref, m_ref) in enumerate(((x_ref, bt_ref), (dy_ref, ct_ref))):
        m = m_ref[...]
        states = []
        for k in range(2):
            cum = cum_ref[k]
            scale = jnp.exp(cum[ROWS - 1 : ROWS, :] - cum if way == 0 else cum)
            high, low_part = halves(v_ref[:, k * GC : (k + 1) * GC].astype(F32) * spread(scale))
            states.append(dot(m, high) + dot(m, low_part))
        keep_ref[0, way] = jnp.where(low, states[0], states[1])
        send_ref[0, way] = jnp.where(low, states[1], states[0])


def chunk_states(place, x, dy, cum, bt, ct):
    columns = pl.BlockSpec((ROWS, 2 * GC), lambda s, place: (0, s))
    whole = pl.BlockSpec((N, ROWS), lambda s, place: (0, 0))
    quad = pl.BlockSpec((1, *PAIR), lambda s, place: (s, 0, 0, 0))
    return pl.pallas_call(
        states_kernel,
        grid_spec=pltpu.PrefetchScalarGridSpec(
            num_scalar_prefetch=1,
            grid=(CHIPS,),
            in_specs=[
                columns,
                columns,
                pl.BlockSpec((2, ROWS, 16), lambda s, place: (s, 0, 0)),
                whole,
                whole,
            ],
            out_specs=[quad, quad],
        ),
        out_shape=[jax.ShapeDtypeStruct((CHIPS, *PAIR), F32)] * 2,
        compiler_params=pltpu.CompilerParams(vmem_limit_bytes=60 << 20),
        name="chunk_states",
    )(place, x, dy, cum, bt, ct)


def join_kernel(place_ref, keep_ref, come_ref, kept_ref, *outs):
    low = place_ref[0] == 0
    for turn, out in enumerate(outs):
        j = lax.rem(place_ref[1] + turn, CHIPS)
        for way in range(2):
            scaled = low if way == 0 else jnp.logical_not(low)
            keep, come = keep_ref[j, way], come_ref[j, way]
            out[way] = jnp.where(scaled, keep, come) * kept_ref[1 - way, j] + jnp.where(
                scaled, come, keep
            )


ORDERS = ((0, 1, 2, 3), (3, 2, 1, 0))


def totals_kernel(place_ref, r0, r1, r2, r3, d_ref, out_ref, sorted_ref):
    for turn, ref in enumerate((r0, r1, r2, r3)):
        sorted_ref[lax.rem(place_ref[1] - turn + CHIPS, CHIPS)] = ref[...]
    for way, order in enumerate(ORDERS):
        total = sorted_ref[order[0], way]
        for c in order[1:]:
            total = total * d_ref[c : c + 1, :] + sorted_ref[c, way]
        out_ref[16 * way : 16 * way + 16, :, :GC] = total.reshape(16, 8, GC)
    for tile in range(PAIRS):
        row = d_ref[CHIPS : CHIPS + 1, 128 * tile : 128 * tile + 128]
        out_ref[:, tile : tile + 1, GC:] = jnp.broadcast_to(row[None], (32, 1, 128))
    out_ref[:, PAIRS:, GC:] = jnp.zeros((32, 8 - PAIRS, 128), F32)


def chain_kernel(flag_ref, p_ref, out_ref):
    backward = flag_ref[0] == 1
    state = [jnp.zeros((8, 128), F32) for _ in range(PAIRS)]
    for s in range(32):
        k = jnp.where(backward, 31 - s, s)
        for t in range(PAIRS):
            columns = slice(128 * t, 128 * t + 128)
            out_ref[k, :, columns] = state[t]
            state[t] = state[t] * p_ref[k, t : t + 1, GC:] + p_ref[k, :, columns]


def entering_kernel(place_ref, sorted_ref, d_ref, edge_ref, o0, o1, o2, o3, all_ref):
    for way, order in enumerate(ORDERS):
        e = edge_ref[16 * way : 16 * way + 16].reshape(N, GC)
        for c in order:
            all_ref[c, way] = e
            if c != order[-1]:
                e = e * d_ref[c : c + 1, :] + sorted_ref[c, way]
    for turn, out in enumerate((o0, o1, o2, o3)):
        at = lax.rem(place_ref[1] + turn, CHIPS)
        for way in range(2):
            high, low = halves(all_ref[at, way])
            out[way, :N] = high
            out[way, N:] = low[:LOWS]


def fork_kernel(place, r_ref, keep_ref, come_ref, kept_ref, mine_ref, send_ref):
    low = place[0] == 0
    for way in range(2):
        direct_is_mine = low if way == 0 else jnp.logical_not(low)
        low_rows = jnp.concatenate(
            [r_ref[way, N:].astype(F32), jnp.zeros((N - LOWS, GC), F32)], axis=0
        )
        direct = r_ref[way, :N].astype(F32) + low_rows
        passed = jnp.where(direct_is_mine, keep_ref[0, way], come_ref[0, way])
        through = kept_ref[way, 0] * direct + passed
        mine_ref[way] = jnp.where(direct_is_mine, direct, through)
        send_ref[way] = jnp.where(direct_is_mine, through, direct)


def fork(turn, place, r, keep, come, kept):
    source = lambda place: lax.rem(place[1] - turn + CHIPS, CHIPS)
    quad = pl.BlockSpec((1, *PAIR), lambda s, place: (source(place), 0, 0, 0))
    pair = pl.BlockSpec(PAIR, lambda s, place: (0, 0, 0))
    return pl.pallas_call(
        fork_kernel,
        grid_spec=pltpu.PrefetchScalarGridSpec(
            num_scalar_prefetch=1,
            grid=(1,),
            in_specs=[
                pl.BlockSpec((2, N + LOWS, GC), lambda s, place: (0, 0, 0)),
                quad,
                quad,
                pl.BlockSpec((2, 1, 1, GC), lambda s, place: (0, source(place), 0, 0)),
            ],
            out_specs=[pair, pair],
        ),
        out_shape=[jax.ShapeDtypeStruct(PAIR, F32)] * 2,
        compiler_params=pltpu.CompilerParams(vmem_limit_bytes=40 << 20),
        name="fork",
    )(place, r, keep, come, kept)


def finish_kernel(
    place, x_ref, dy_ref, cum_ref, y_ref, dx_ref, m0, m1, m2, m3, c0, c1, c2, c3, gain_ref, b_ref, c_ref,
    db0_ref, dc0_ref, out_ref, gs_ref, o0, o1, o2, o3, db_ref, dc_ref, gd_ref, mine_ref, come_ref,
):
    step = pl.program_id(0)
    low_core = place[0] == 0

    @pl.when(step == 0)
    def _():
        db_ref[...] = db0_ref[...]
        dc_ref[...] = dc0_ref[...]

    for turn, (mine_in, come_in) in enumerate(((m0, c0), (m1, c1), (m2, c2), (m3, c3))):

        @pl.when(step == turn)
        def _(mine_in=mine_in, come_in=come_in):
            mine_ref[...] = mine_in[...]
            come_ref[...] = come_in[...]

    def both(way):
        mine, come = mine_ref[way], come_ref[way]
        return jnp.concatenate([jnp.where(low_core, mine, come), jnp.where(low_core, come, mine)], axis=1)

    cums = cum_ref[0], cum_ref[1]
    from_start = jnp.concatenate([spread(jnp.exp(v)) for v in cums], axis=1)
    to_end = jnp.concatenate([spread(jnp.exp(v[ROWS - 1 : ROWS, :] - v)) for v in cums], axis=1)
    gain = jnp.concatenate([gain_ref[0], gain_ref[1]], axis=1)
    x = x_ref[...].astype(F32)
    dy = dy_ref[...].astype(F32)
    entering, leaving = both(0), both(1)
    b, c = b_ref[...], c_ref[...]

    def carried(matrix, state, scale, v):
        parts = jnp.concatenate(halves(state), axis=0)
        product = scale * dot(jnp.concatenate([matrix, matrix], axis=1), parts)
        high, low = halves(scale * v)
        wide = dot(high, parts, NT)
        return product, wide[:, :N] + wide[:, N:] + dot(low, parts[:N], NT)

    y_carried, dc = carried(c, entering, from_start, dy)
    dx_carried, db = carried(b, leaving, to_end, x)
    y = y_ref[...] + y_carried
    dx_in = dx_ref[...]
    out_ref[...] = (y + gain * x).astype(BF16)
    gs_ref[...] = (dx_in + dx_carried + gain * dy).astype(BF16)
    dc_ref[...] += dc
    db_ref[...] += db
    of_head = (
        lax.broadcasted_iota(jnp.int32, (32, 2 * GC), 1) // GC * 16
        + lax.broadcasted_iota(jnp.int32, (32, 2 * GC), 1) % GC // HEAD
        == lax.broadcasted_iota(jnp.int32, (32, 2 * GC), 0)
    ).astype(BF16)

    def by_head(v):
        high, low = halves(v)
        return dot(of_head, high, NT) + dot(of_head, low, NT)

    x_dx = x * dx_carried
    row = from_start[ROWS - 1 : ROWS, :] * jnp.sum(entering * leaving, axis=0, keepdims=True)
    row += jnp.sum(x_dx, axis=0, keepdims=True)
    t = lax.broadcasted_iota(jnp.int32, (ROWS, ROWS), 0)
    s = lax.broadcasted_iota(jnp.int32, (ROWS, ROWS), 1)
    after = (t >= s).astype(BF16)
    gd = jnp.broadcast_to(by_head(jnp.broadcast_to(row, (8, 2 * GC)))[:, 0:1], (32, ROWS))
    for part in thirds(by_head(dy * y - (x * dx_in + x_dx))):
        gd += dot(part, after)
    gd_ref[lax.rem(place[1] - step + CHIPS, CHIPS)] = gd

    @pl.when(step == CHIPS - 1)
    def _():
        for turn, out in enumerate((o0, o1, o2, o3)):
            out[0:ROWS, :] = db_ref[...]
            out[ROWS : 2 * ROWS, :] = dc_ref[...]
            mine = gd_ref[lax.rem(place[1] + turn, CHIPS)]
            out[384:416, :] = mine[:, 0:128]
            out[416:448, 0:64] = mine[:, 128:192]
            out[416:448, 64:128] = jnp.zeros((32, 64), F32)


def finish(place, x, dy, cum, y, dx, mine, come, gain, b, c, db, dc):
    source = lambda s, place: lax.rem(place[1] - s + CHIPS, CHIPS)
    columns = pl.BlockSpec((ROWS, 2 * GC), lambda s, place: (0, source(s, place)))
    by_chip = lambda *shape: pl.BlockSpec((2, *shape), lambda s, place: (source(s, place), 0, 0))
    pair = pl.BlockSpec(PAIR, lambda s, place: (0, 0, 0))
    whole = lambda *shape: pl.BlockSpec(shape, lambda s, place: (0, 0))
    wide = jax.ShapeDtypeStruct((ROWS, GC * GROUPS), BF16)
    return pl.pallas_call(
        finish_kernel,
        grid_spec=pltpu.PrefetchScalarGridSpec(
            num_scalar_prefetch=1,
            grid=(CHIPS,),
            in_specs=[
                columns, columns, by_chip(ROWS, 16), columns, columns, *[pair] * 8,
                by_chip(1, GC), *[whole(ROWS, N)] * 4,
            ],
            out_specs=[columns, columns] + [whole(448, 128)] * 4,
            scratch_shapes=[
                pltpu.VMEM((ROWS, N), F32), pltpu.VMEM((ROWS, N), F32), pltpu.VMEM((CHIPS, 32, ROWS), F32),
                pltpu.VMEM(PAIR, F32), pltpu.VMEM(PAIR, F32),
            ],
        ),
        out_shape=[wide, wide] + [jax.ShapeDtypeStruct((448, 128), F32)] * 4,
        compiler_params=pltpu.CompilerParams(vmem_limit_bytes=60 << 20),
        name="finish",
    )(place, x, dy, cum, y, dx, *mine, *come, gain, b, c, db, dc)


def tie(*values):
    return lax.optimization_barrier(values)


def turned(v):
    r = {
        turn: lax.ppermute(v[turn], "y", [(i, (i + turn) % CHIPS) for i in range(CHIPS)])
        for turn in (2, 1, 3)
    }
    return [v[0], r[1], r[2], r[3]]


def gathered(parts, iy, low):
    by_chip = jnp.roll(jnp.stack([parts[0], parts[3], parts[2], parts[1]]), iy, axis=0)
    other = lax.ppermute(by_chip, "core", SWAP)
    return jnp.stack(
        [jnp.where(low, by_chip, other), jnp.where(low, other, by_chip)], axis=1
    ).reshape(GROUPS, *by_chip.shape[1:])


def shards(x, dy, b_all, c_all, log_decay, skip_gain):
    ix = lax.axis_index("x")
    iy, core = lax.axis_index("y"), lax.axis_index("core")
    place = jnp.stack([core, iy]).astype(jnp.int32)
    row0 = (2 * iy + core) * ROWS
    b = lax.dynamic_slice_in_dim(b_all, row0, ROWS, 0)
    c = lax.dynamic_slice_in_dim(c_all, row0, ROWS, 0)
    swap = lambda v: lax.ppermute(v, "core", SWAP)
    over_ctx = lambda v: lax.all_to_all(v, ("x", "z"), split_axis=0, concat_axis=0, tiled=True)
    pair = lambda dtype: jax.ShapeDtypeStruct(PAIR, dtype)
    quad = jax.ShapeDtypeStruct((CHIPS, *PAIR), F32)

    ldt = log_decay.T
    [packed] = on_chip(
        pack_kernel, "pack", [jax.ShapeDtypeStruct((GROUPS, 2, 16, ROWS), F32)],
        ldt, skip_gain.reshape(1, HG), scalars=0,
    )
    got = lax.all_to_all(packed, ("y", "core"), split_axis=0, concat_axis=0, tiled=True)
    cumt, cum, gain, kept = on_chip(
        decays_kernel, "decays",
        [
            jax.ShapeDtypeStruct((GROUPS, 16, ROWS), F32),
            jax.ShapeDtypeStruct((GROUPS, ROWS, 16), F32),
            jax.ShapeDtypeStruct((GROUPS, 1, GC), F32),
            jax.ShapeDtypeStruct((2, CHIPS, 1, GC), F32),
        ],
        place, got,
    )
    send, keep = chunk_states(place, x, dy, cum, b.T, c.T)
    come = swap(send)
    out = on_chip(join_kernel, "join", [pair(F32)] * 4, place, keep, come, kept)
    parts = turned(out)
    x_w, dy_w, ldt_w, _ = tie(x, dy, ldt, out[0])
    [own] = on_chip(owner_kernel, "owner_decays", [jax.ShapeDtypeStruct((8, GC), F32)], ldt_w, scalars=0)
    inside = within(x_w, dy_w, cum, cumt, b, c)
    y_in, dx_in, db_in, dc_in, *parts = tie(*inside, *parts)
    total, by_chip = on_chip(
        totals_kernel, "totals", [jax.ShapeDtypeStruct((32, 8, GC + 128), F32), quad], place, *parts, own
    )
    total = over_ctx(total)
    flag = (ix >= 2).reshape(1).astype(jnp.int32)
    [edge] = on_chip(
        chain_kernel, "chain", [jax.ShapeDtypeStruct((32, 8, GC), F32)], flag, total
    )
    edge = over_ctx(edge)
    out = on_chip(
        entering_kernel, "entering", [jax.ShapeDtypeStruct((2, N + LOWS, GC), BF16)] * 4, place, by_chip, own, edge,
        scratch=[pltpu.VMEM((CHIPS, *PAIR), F32)],
    )
    mine, come_in = [], []
    for turn, r in enumerate(turned(out)):
        own_part, send = fork(turn, place, r, keep, come, kept)
        mine.append(own_part)
        come_in.append(swap(send))
    scan_out, grad_x, *ends = finish(
        place, x, dy, cum, y_in, dx_in, mine, come_in, gain, b, c, db_in, dc_in
    )
    ends = gathered(turned(ends), iy, core == 0)
    grad_b = ends[:, :ROWS].reshape(GROUPS * ROWS, N)
    grad_c = ends[:, ROWS : 2 * ROWS].reshape(GROUPS * ROWS, N)
    rest = ends[:, 2 * ROWS :].reshape(GROUPS, 2, 2, 16, 128)
    rest = lax.dynamic_index_in_dim(rest, core, 2, keepdims=False)
    rest = jnp.concatenate([rest[:, 0, :HG], rest[:, 1, :HG, :64]], axis=2)
    grad_decay = rest.transpose(0, 2, 1).reshape(GROUPS * ROWS, HG)
    return scan_out, grad_x, grad_b, grad_c, grad_decay


def solution(mesh):
    grid = Mesh(mesh.devices.reshape(4, 8, 4, 2), ("x", "z", "y", "core"))
    ctx, head = ("x", "z"), ("y", "core")
    rows = P((*ctx, *head), None)
    return jax.shard_map(
        shards,
        mesh=grid,
        in_specs=(rows, rows, P(ctx, None), P(ctx, None), P(ctx, head), P(head)),
        out_specs=(rows, rows, P(ctx, None), P(ctx, None), P(ctx, head)),
        check_vma=False,
    )
```

```python
import functools

import jax
import jax.numpy as jnp
from jax import lax
from jax.experimental import pallas as pl
from jax.experimental.pallas import tpu as pltpu
from jax.sharding import Mesh
from jax.sharding import PartitionSpec as P

ROWS = 192
N = 128
HEAD = 64
HG = 10
GC = HG * HEAD
GROUPS = 8
PAIRS = GC // 128
F32, BF16 = jnp.float32, jnp.bfloat16
SWAP = [(0, 1), (1, 0)]
NN = (((1,), (0,)), ((), ()))
NT = (((1,), (1,)), ((), ()))
TN = (((0,), (0,)), ((), ()))


def dot(a, b, dims=NN):
    return lax.dot_general(a, b, dims, preferred_element_type=F32)


def halves(v):
    high = v.astype(BF16)
    return high, (v - high.astype(F32)).astype(BF16)


def thirds(v):
    high = v.astype(BF16)
    rest = v - high.astype(F32)
    middle = rest.astype(BF16)
    return high, middle, (rest - middle.astype(F32)).astype(BF16)


def spread(columns):
    rows = columns.shape[0]
    first = lax.broadcasted_iota(jnp.int32, (rows, 128), 1) < HEAD
    return jnp.concatenate(
        [
            jnp.where(
                first,
                jnp.broadcast_to(columns[:, 2 * p : 2 * p + 1], (rows, 128)),
                jnp.broadcast_to(columns[:, 2 * p + 1 : 2 * p + 2], (rows, 128)),
            )
            for p in range(PAIRS)
        ],
        axis=1,
    )


def within_kernel(
    x_ref, dy_ref, cum_ref, cumt_ref, b_ref, c_ref, y_ref, dx_ref, db_ref, dc_ref, score_ref, acc_ref
):
    step = pl.program_id(0)
    causal = lax.broadcasted_iota(jnp.int32, (ROWS, ROWS), 0) >= lax.broadcasted_iota(
        jnp.int32, (ROWS, ROWS), 1
    )

    @pl.when(step == 0)
    def _():
        score_ref[...] = jnp.where(causal, dot(c_ref[...], b_ref[...], NT), 0.0)
        acc_ref[...] = jnp.zeros_like(acc_ref)

    first = lax.broadcasted_iota(jnp.int32, (ROWS, 128), 1) < HEAD
    zero = jnp.zeros((ROWS, 128), BF16)
    for p in range(PAIRS):
        columns = slice(128 * p, 128 * p + 128)
        x = x_ref[:, columns]
        dy = dy_ref[:, columns]
        y = dx = None
        for side in range(2):
            h = 2 * p + side
            keep = first if side == 0 else jnp.logical_not(first)
            xs = jnp.where(keep, x, zero)
            dys = jnp.where(keep, dy, zero)
            decay = jnp.exp(
                jnp.minimum(cum_ref[0, :, h : h + 1] - cumt_ref[0, h : h + 1, :], 0.0)
            )
            weights = (score_ref[...] * decay).astype(BF16)
            part = dot(weights, xs)
            y = part if y is None else y + part
            dweights = dot(dys, x, NT).astype(BF16).astype(F32)
            acc_ref[...] += dweights * decay
            part = dot(weights, dys, TN)
            dx = part if dx is None else dx + part
        y_ref[:, columns] = y
        dx_ref[:, columns] = dx

    @pl.when(step == GROUPS - 1)
    def _():
        high, low = halves(jnp.where(causal, acc_ref[...], 0.0))
        b, c = b_ref[...], c_ref[...]
        dc_ref[...] = dot(high, b) + dot(low, b)
        db_ref[...] = dot(high, c, TN) + dot(low, c, TN)


def within(x, dy, cum, cumt, b, c):
    by_column = pl.BlockSpec((ROWS, GC), lambda s: (0, s))
    whole = pl.BlockSpec((ROWS, N), lambda s: (0, 0))
    wide = jax.ShapeDtypeStruct((ROWS, GC * GROUPS), F32)
    small = jax.ShapeDtypeStruct((ROWS, N), F32)
    return pl.pallas_call(
        within_kernel,
        grid=(GROUPS,),
        in_specs=[
            by_column,
            by_column,
            pl.BlockSpec((1, ROWS, 16), lambda s: (s, 0, 0)),
            pl.BlockSpec((1, 16, ROWS), lambda s: (s, 0, 0)),
            whole,
            whole,
        ],
        out_specs=[by_column, by_column, whole, whole],
        out_shape=[wide, wide, small, small],
        scratch_shapes=[pltpu.VMEM((ROWS, ROWS), F32), pltpu.VMEM((ROWS, ROWS), F32)],
        compiler_params=pltpu.CompilerParams(vmem_limit_bytes=40 << 20),
        cost_estimate=pl.CostEstimate(
            flops=20_000_000_000, bytes_accessed=12_000_000, transcendentals=3_000_000
        ),
        name="within_chunk",
    )(x, dy, cum, cumt, b, c)


CHIPS = 4
VMEM = pl.BlockSpec(memory_space=pltpu.VMEM)
SMEM = pl.BlockSpec(memory_space=pltpu.SMEM)
PAIR = (2, N, GC)
LOWS = 64


def on_chip(kernel, name, outs, *args, scratch=(), scalars=1):
    return pl.pallas_call(
        kernel,
        in_specs=[SMEM] * scalars + [VMEM] * (len(args) - scalars),
        out_specs=[VMEM] * len(outs),
        out_shape=outs,
        scratch_shapes=list(scratch),
        compiler_params=pltpu.CompilerParams(vmem_limit_bytes=44 << 20),
        name=name,
    )(*args)


def pack_kernel(ld_ref, gain_ref, out_ref):
    out_ref[...] = jnp.zeros_like(out_ref)
    for chunk in range(GROUPS):
        rows = ld_ref[:, chunk * ROWS : (chunk + 1) * ROWS]
        for core in range(2):
            at = 2 * (chunk // 2) + core
            out_ref[at, chunk % 2, 0:HG, :] = rows
            out_ref[at, chunk % 2, HG : HG + 1, 0:HG] = gain_ref[...]


def owner_kernel(ld_ref, out_ref):
    width = 2 * ROWS
    of = lax.broadcasted_iota(jnp.int32, (8, 8 * ROWS), 1) // width
    row = lax.broadcasted_iota(jnp.int32, (8, 8 * ROWS), 0)
    pick = jnp.logical_or(of == row, row == CHIPS).astype(BF16)
    totals = sum(dot(pick, part, NT) for part in thirds(ld_ref[...]))
    out_ref[...] = spread(jnp.exp(totals))


def decays_kernel(core_ref, got_ref, cumt_ref, cum_ref, gain_ref, kept_ref):
    low = core_ref[0] == 0
    t = lax.broadcasted_iota(jnp.int32, (ROWS, ROWS), 0)
    s = lax.broadcasted_iota(jnp.int32, (ROWS, ROWS), 1)
    upper = (t <= s).astype(BF16)
    lower = (t >= s).astype(BF16)
    is_head = lax.broadcasted_iota(jnp.int32, (GROUPS, 16, ROWS), 1) < HG
    flat, tall = [], []
    for half in range(2):
        ld = jnp.where(is_head, got_ref[:, half], 0.0).reshape(GROUPS * 16, ROWS)
        parts = thirds(ld)
        flat.append(sum(dot(part, upper) for part in parts))
        tall.append(sum(dot(lower, part, NT) for part in parts))
    cumt_ref[...] = jnp.where(low, flat[0], flat[1]).reshape(GROUPS, 16, ROWS)
    own = jnp.where(low, tall[0], tall[1])
    for g in range(GROUPS):
        cum_ref[g] = own[:, 16 * g : 16 * g + 16]
        gain_ref[g] = spread(got_ref[g, 0, HG : HG + 1, :])
    for half in range(2):
        ends = jnp.exp(tall[half][ROWS - 1 : ROWS, :])
        for j in range(CHIPS):
            a = ends[:, 32 * j : 32 * j + 16]
            b = ends[:, 32 * j + 16 : 32 * j + 32]
            kept_ref[half, j] = spread(jnp.where(low, a, b))


def states_kernel(place, x_ref, dy_ref, cum_ref, bt_ref, ct_ref, send_ref, keep_ref):
    low = place[0] == 0
    for way, (v_ref, m_ref) in enumerate(((x_ref, bt_ref), (dy_ref, ct_ref))):
        m = m_ref[...]
        states = []
        for k in range(2):
            cum = cum_ref[k]
            scale = jnp.exp(cum[ROWS - 1 : ROWS, :] - cum if way == 0 else cum)
            high, low_part = halves(v_ref[:, k * GC : (k + 1) * GC].astype(F32) * spread(scale))
            states.append(dot(m, high) + dot(m, low_part))
        keep_ref[0, way] = jnp.where(low, states[0], states[1])
        send_ref[0, way] = jnp.where(low, states[1], states[0])


def chunk_states(place, x, dy, cum, bt, ct):
    columns = pl.BlockSpec((ROWS, 2 * GC), lambda s, place: (0, s))
    whole = pl.BlockSpec((N, ROWS), lambda s, place: (0, 0))
    quad = pl.BlockSpec((1, *PAIR), lambda s, place: (s, 0, 0, 0))
    return pl.pallas_call(
        states_kernel,
        grid_spec=pltpu.PrefetchScalarGridSpec(
            num_scalar_prefetch=1,
            grid=(CHIPS,),
            in_specs=[
                columns,
                columns,
                pl.BlockSpec((2, ROWS, 16), lambda s, place: (s, 0, 0)),
                whole,
                whole,
            ],
            out_specs=[quad, quad],
        ),
        out_shape=[jax.ShapeDtypeStruct((CHIPS, *PAIR), F32)] * 2,
        compiler_params=pltpu.CompilerParams(vmem_limit_bytes=40 << 20),
        name="chunk_states",
    )(place, x, dy, cum, bt, ct)


def join_kernel(place_ref, keep_ref, come_ref, kept_ref, *outs):
    low = place_ref[0] == 0
    for turn, out in enumerate(outs):
        j = lax.rem(place_ref[1] + turn, CHIPS)
        for way in range(2):
            scaled = low if way == 0 else jnp.logical_not(low)
            keep, come = keep_ref[j, way], come_ref[j, way]
            out[way] = jnp.where(scaled, keep, come) * kept_ref[1 - way, j] + jnp.where(
                scaled, come, keep
            )


ORDERS = ((0, 1, 2, 3), (3, 2, 1, 0))


def totals_kernel(place_ref, r0, r1, r2, r3, d_ref, out_ref, sorted_ref):
    for turn, ref in enumerate((r0, r1, r2, r3)):
        sorted_ref[lax.rem(place_ref[1] - turn + CHIPS, CHIPS)] = ref[...]
    for way, order in enumerate(ORDERS):
        total = sorted_ref[order[0], way]
        for c in order[1:]:
            total = total * d_ref[c : c + 1, :] + sorted_ref[c, way]
        out_ref[16 * way : 16 * way + 16, :, :GC] = total.reshape(16, 8, GC)
    for tile in range(PAIRS):
        row = d_ref[CHIPS : CHIPS + 1, 128 * tile : 128 * tile + 128]
        out_ref[:, tile : tile + 1, GC:] = jnp.broadcast_to(row[None], (32, 1, 128))
    out_ref[:, PAIRS:, GC:] = jnp.zeros((32, 8 - PAIRS, 128), F32)


def chain_kernel(flag_ref, p_ref, out_ref):
    backward = flag_ref[0] == 1
    state = [jnp.zeros((8, 128), F32) for _ in range(PAIRS)]
    for s in range(32):
        k = jnp.where(backward, 31 - s, s)
        for t in range(PAIRS):
            columns = slice(128 * t, 128 * t + 128)
            out_ref[k, :, columns] = state[t]
            state[t] = state[t] * p_ref[k, t : t + 1, GC:] + p_ref[k, :, columns]


def entering_kernel(place_ref, sorted_ref, d_ref, edge_ref, o0, o1, o2, o3, all_ref):
    for way, order in enumerate(ORDERS):
        e = edge_ref[16 * way : 16 * way + 16].reshape(N, GC)
        for c in order:
            all_ref[c, way] = e
            if c != order[-1]:
                e = e * d_ref[c : c + 1, :] + sorted_ref[c, way]
    for turn, out in enumerate((o0, o1, o2, o3)):
        at = lax.rem(place_ref[1] + turn, CHIPS)
        for way in range(2):
            high, low = halves(all_ref[at, way])
            out[way, :N] = high
            out[way, N:] = low[:LOWS]


def fork_kernel(place_ref, r0, r1, r2, r3, keep_ref, come_ref, kept_ref, mine_ref, send_ref):
    low = place_ref[0] == 0
    for turn, ref in enumerate((r0, r1, r2, r3)):
        j = lax.rem(place_ref[1] - turn + CHIPS, CHIPS)
        for way in range(2):
            direct_is_mine = low if way == 0 else jnp.logical_not(low)
            low_rows = jnp.concatenate(
                [ref[way, N:].astype(F32), jnp.zeros((N - LOWS, GC), F32)], axis=0
            )
            direct = ref[way, :N].astype(F32) + low_rows
            passed = jnp.where(direct_is_mine, keep_ref[j, way], come_ref[j, way])
            through = kept_ref[way, j] * direct + passed
            mine_ref[j, way] = jnp.where(direct_is_mine, direct, through)
            send_ref[j, way] = jnp.where(direct_is_mine, through, direct)


def finish_kernel(
    place, x_ref, dy_ref, cum_ref, cumt_ref, y_ref, dx_ref, mine_ref, come_ref, gain_ref, b_ref, c_ref,
    db0_ref, dc0_ref, out_ref, gs_ref, o0, o1, o2, o3, db_ref, dc_ref, gd_ref,
):
    step = pl.program_id(0)
    low_core = place[0] == 0

    @pl.when(step == 0)
    def _():
        db_ref[...] = db0_ref[...]
        dc_ref[...] = dc0_ref[...]

    def both(way):
        mine, come = mine_ref[0, way], come_ref[0, way]
        return jnp.concatenate([jnp.where(low_core, mine, come), jnp.where(low_core, come, mine)], axis=1)

    cums = cum_ref[0], cum_ref[1]
    from_start = jnp.concatenate([spread(jnp.exp(v)) for v in cums], axis=1)
    to_end = jnp.concatenate([spread(jnp.exp(v[ROWS - 1 : ROWS, :] - v)) for v in cums], axis=1)
    gain = jnp.concatenate([gain_ref[0], gain_ref[1]], axis=1)
    x = x_ref[...].astype(F32)
    dy = dy_ref[...].astype(F32)
    entering, leaving = both(0), both(1)
    b, c = b_ref[...], c_ref[...]

    def carried(matrix, state, scale, v):
        parts = jnp.concatenate(halves(state), axis=0)
        product = scale * dot(jnp.concatenate([matrix, matrix], axis=1), parts)
        high, low = halves(scale * v)
        wide = dot(high, parts, NT)
        return product, wide[:, :N] + wide[:, N:] + dot(low, parts[:N], NT)

    y_carried, dc = carried(c, entering, from_start, dy)
    dx_carried, db = carried(b, leaving, to_end, x)
    y = y_ref[...] + y_carried
    dx_in = dx_ref[...]
    out_ref[...] = (y + gain * x).astype(BF16)
    gs_ref[...] = (dx_in + dx_carried + gain * dy).astype(BF16)
    dc_ref[...] += dc
    db_ref[...] += db
    of_head = (
        lax.broadcasted_iota(jnp.int32, (32, 2 * GC), 1) // GC * 16
        + lax.broadcasted_iota(jnp.int32, (32, 2 * GC), 1) % GC // HEAD
        == lax.broadcasted_iota(jnp.int32, (32, 2 * GC), 0)
    ).astype(BF16)

    def by_head(v):
        high, low = halves(v)
        return dot(of_head, high, NT) + dot(of_head, low, NT)

    x_dx = x * dx_carried
    row = from_start[ROWS - 1 : ROWS, :] * jnp.sum(entering * leaving, axis=0, keepdims=True)
    row += jnp.sum(x_dx, axis=0, keepdims=True)
    t = lax.broadcasted_iota(jnp.int32, (ROWS, ROWS), 0)
    s = lax.broadcasted_iota(jnp.int32, (ROWS, ROWS), 1)
    after = (t >= s).astype(BF16)
    gd = jnp.broadcast_to(by_head(jnp.broadcast_to(row, (8, 2 * GC)))[:, 0:1], (32, ROWS))
    for part in thirds(by_head(dy * y - (x * dx_in + x_dx))):
        gd += dot(part, after)
    gd_ref[step] = gd

    @pl.when(step == CHIPS - 1)
    def _():
        for turn, out in enumerate((o0, o1, o2, o3)):
            out[0:ROWS, :] = db_ref[...]
            out[ROWS : 2 * ROWS, :] = dc_ref[...]
            mine = gd_ref[lax.rem(place[1] + turn, CHIPS)]
            out[384:416, :] = mine[:, 0:128]
            out[416:448, 0:64] = mine[:, 128:192]
            out[416:448, 64:128] = jnp.zeros((32, 64), F32)


def finish(place, x, dy, cum, cumt, y, dx, mine, come, gain, b, c, db, dc):
    columns = pl.BlockSpec((ROWS, 2 * GC), lambda s, place: (0, s))
    by_chip = lambda *shape: pl.BlockSpec((2, *shape), lambda s, place: (s, 0, 0))
    quad = pl.BlockSpec((1, *PAIR), lambda s, place: (s, 0, 0, 0))
    whole = lambda *shape: pl.BlockSpec(shape, lambda s, place: (0, 0))
    wide = jax.ShapeDtypeStruct((ROWS, GC * GROUPS), BF16)
    return pl.pallas_call(
        finish_kernel,
        grid_spec=pltpu.PrefetchScalarGridSpec(
            num_scalar_prefetch=1,
            grid=(CHIPS,),
            in_specs=[
                columns, columns, by_chip(ROWS, 16), by_chip(16, ROWS), columns, columns, quad, quad,
                by_chip(1, GC), *[whole(ROWS, N)] * 4,
            ],
            out_specs=[columns, columns] + [whole(448, 128)] * 4,
            scratch_shapes=[
                pltpu.VMEM((ROWS, N), F32), pltpu.VMEM((ROWS, N), F32), pltpu.VMEM((CHIPS, 32, ROWS), F32),
            ],
        ),
        out_shape=[wide, wide] + [jax.ShapeDtypeStruct((448, 128), F32)] * 4,
        compiler_params=pltpu.CompilerParams(vmem_limit_bytes=60 << 20),
        name="finish",
    )(place, x, dy, cum, cumt, y, dx, mine, come, gain, b, c, db, dc)


def tie(*values):
    return lax.optimization_barrier(values)


def turned(v):
    r = {
        turn: lax.ppermute(v[turn], "y", [(i, (i + turn) % CHIPS) for i in range(CHIPS)])
        for turn in (2, 1, 3)
    }
    return [v[0], r[1], r[2], r[3]]


def gathered(parts, iy, low):
    by_chip = jnp.roll(jnp.stack([parts[0], parts[3], parts[2], parts[1]]), iy, axis=0)
    other = lax.ppermute(by_chip, "core", SWAP)
    return jnp.stack(
        [jnp.where(low, by_chip, other), jnp.where(low, other, by_chip)], axis=1
    ).reshape(GROUPS, *by_chip.shape[1:])


def shards(x, dy, b_all, c_all, log_decay, skip_gain):
    ix = lax.axis_index("x")
    iy, core = lax.axis_index("y"), lax.axis_index("core")
    place = jnp.stack([core, iy]).astype(jnp.int32)
    row0 = (2 * iy + core) * ROWS
    b = lax.dynamic_slice_in_dim(b_all, row0, ROWS, 0)
    c = lax.dynamic_slice_in_dim(c_all, row0, ROWS, 0)
    swap = lambda v: lax.ppermute(v, "core", SWAP)
    over_ctx = lambda v: lax.all_to_all(v, ("x", "z"), split_axis=0, concat_axis=0, tiled=True)
    pair = lambda dtype: jax.ShapeDtypeStruct(PAIR, dtype)
    quad = jax.ShapeDtypeStruct((CHIPS, *PAIR), F32)

    ldt = log_decay.T
    [packed] = on_chip(
        pack_kernel, "pack", [jax.ShapeDtypeStruct((GROUPS, 2, 16, ROWS), F32)],
        ldt, skip_gain.reshape(1, HG), scalars=0,
    )
    got = lax.all_to_all(packed, ("y", "core"), split_axis=0, concat_axis=0, tiled=True)
    cumt, cum, gain, kept = on_chip(
        decays_kernel, "decays",
        [
            jax.ShapeDtypeStruct((GROUPS, 16, ROWS), F32),
            jax.ShapeDtypeStruct((GROUPS, ROWS, 16), F32),
            jax.ShapeDtypeStruct((GROUPS, 1, GC), F32),
            jax.ShapeDtypeStruct((2, CHIPS, 1, GC), F32),
        ],
        place, got,
    )
    send, keep = chunk_states(place, x, dy, cum, b.T, c.T)
    come = swap(send)
    out = on_chip(join_kernel, "join", [pair(F32)] * 4, place, keep, come, kept)
    parts = turned(out)
    x_w, dy_w, ldt_w, _ = tie(x, dy, ldt, out[0])
    [own] = on_chip(owner_kernel, "owner_decays", [jax.ShapeDtypeStruct((8, GC), F32)], ldt_w, scalars=0)
    inside = within(x_w, dy_w, cum, cumt, b, c)
    y_in, dx_in, db_in, dc_in, *parts = tie(*inside, *parts)
    total, by_chip = on_chip(
        totals_kernel, "totals", [jax.ShapeDtypeStruct((32, 8, GC + 128), F32), quad], place, *parts, own
    )
    total = over_ctx(total)
    flag = (ix >= 2).reshape(1).astype(jnp.int32)
    [edge] = on_chip(
        chain_kernel, "chain", [jax.ShapeDtypeStruct((32, 8, GC), F32)], flag, total
    )
    edge = over_ctx(edge)
    out = on_chip(
        entering_kernel, "entering", [jax.ShapeDtypeStruct((2, N + LOWS, GC), BF16)] * 4, place, by_chip, own, edge,
        scratch=[pltpu.VMEM((CHIPS, *PAIR), F32)],
    )
    mine, send = on_chip(fork_kernel, "fork", [quad] * 2, place, *turned(out), keep, come, kept)
    scan_out, grad_x, *ends = finish(
        place, x, dy, cum, cumt, y_in, dx_in, mine, swap(send), gain, b, c, db_in, dc_in
    )
    ends = gathered(turned(ends), iy, core == 0)
    grad_b = ends[:, :ROWS].reshape(GROUPS * ROWS, N)
    grad_c = ends[:, ROWS : 2 * ROWS].reshape(GROUPS * ROWS, N)
    rest = ends[:, 2 * ROWS :].reshape(GROUPS, 2, 2, 16, 128)
    rest = lax.dynamic_index_in_dim(rest, core, 2, keepdims=False)
    rest = jnp.concatenate([rest[:, 0, :HG], rest[:, 1, :HG, :64]], axis=2)
    grad_decay = rest.transpose(0, 2, 1).reshape(GROUPS * ROWS, HG)
    return scan_out, grad_x, grad_b, grad_c, grad_decay


def solution(mesh):
    grid = Mesh(mesh.devices.reshape(4, 8, 4, 2), ("x", "z", "y", "core"))
    ctx, head = ("x", "z"), ("y", "core")
    rows = P((*ctx, *head), None)
    return jax.shard_map(
        shards,
        mesh=grid,
        in_specs=(rows, rows, P(ctx, None), P(ctx, None), P(ctx, head), P(head)),
        out_specs=(rows, rows, P(ctx, None), P(ctx, None), P(ctx, head)),
        check_vma=False,
    )
```

```python
import functools

import jax
import jax.numpy as jnp
from jax import lax
from jax.experimental import pallas as pl
from jax.experimental.pallas import tpu as pltpu
from jax.sharding import Mesh
from jax.sharding import PartitionSpec as P

ROWS = 192
N = 128
HEAD = 64
HG = 10
GC = HG * HEAD
GROUPS = 8
PAIRS = GC // 128
F32, BF16 = jnp.float32, jnp.bfloat16
SWAP = [(0, 1), (1, 0)]
NN = (((1,), (0,)), ((), ()))
NT = (((1,), (1,)), ((), ()))
TN = (((0,), (0,)), ((), ()))


def dot(a, b, dims=NN):
    return lax.dot_general(a, b, dims, preferred_element_type=F32)


def halves(v):
    high = v.astype(BF16)
    return high, (v - high.astype(F32)).astype(BF16)


def thirds(v):
    high = v.astype(BF16)
    rest = v - high.astype(F32)
    middle = rest.astype(BF16)
    return high, middle, (rest - middle.astype(F32)).astype(BF16)


def spread(columns):
    rows = columns.shape[0]
    first = lax.broadcasted_iota(jnp.int32, (rows, 128), 1) < HEAD
    return jnp.concatenate(
        [
            jnp.where(
                first,
                jnp.broadcast_to(columns[:, 2 * p : 2 * p + 1], (rows, 128)),
                jnp.broadcast_to(columns[:, 2 * p + 1 : 2 * p + 2], (rows, 128)),
            )
            for p in range(PAIRS)
        ],
        axis=1,
    )


def within_kernel(
    x_ref, dy_ref, cum_ref, cumt_ref, b_ref, c_ref, y_ref, dx_ref, db_ref, dc_ref, score_ref, acc_ref
):
    step = pl.program_id(0)
    causal = lax.broadcasted_iota(jnp.int32, (ROWS, ROWS), 0) >= lax.broadcasted_iota(
        jnp.int32, (ROWS, ROWS), 1
    )

    @pl.when(step == 0)
    def _():
        score_ref[...] = jnp.where(causal, dot(c_ref[...], b_ref[...], NT), 0.0)
        acc_ref[...] = jnp.zeros_like(acc_ref)

    first = lax.broadcasted_iota(jnp.int32, (ROWS, 128), 1) < HEAD
    zero = jnp.zeros((ROWS, 128), BF16)
    for p in range(PAIRS):
        columns = slice(128 * p, 128 * p + 128)
        x = x_ref[:, columns]
        dy = dy_ref[:, columns]
        y = dx = None
        for side in range(2):
            h = 2 * p + side
            keep = first if side == 0 else jnp.logical_not(first)
            xs = jnp.where(keep, x, zero)
            dys = jnp.where(keep, dy, zero)
            decay = jnp.exp(
                jnp.minimum(cum_ref[0, :, h : h + 1] - cumt_ref[0, h : h + 1, :], 0.0)
            )
            weights = (score_ref[...] * decay).astype(BF16)
            part = dot(weights, xs)
            y = part if y is None else y + part
            dweights = dot(dys, x, NT).astype(BF16).astype(F32)
            acc_ref[...] += dweights * decay
            part = dot(weights, dys, TN)
            dx = part if dx is None else dx + part
        y_ref[:, columns] = y
        dx_ref[:, columns] = dx

    @pl.when(step == GROUPS - 1)
    def _():
        high, low = halves(jnp.where(causal, acc_ref[...], 0.0))
        b, c = b_ref[...], c_ref[...]
        dc_ref[...] = dot(high, b) + dot(low, b)
        db_ref[...] = dot(high, c, TN) + dot(low, c, TN)


def within(x, dy, cum, cumt, b, c):
    by_column = pl.BlockSpec((ROWS, GC), lambda s: (0, s))
    whole = pl.BlockSpec((ROWS, N), lambda s: (0, 0))
    wide = jax.ShapeDtypeStruct((ROWS, GC * GROUPS), F32)
    small = jax.ShapeDtypeStruct((ROWS, N), F32)
    return pl.pallas_call(
        within_kernel,
        grid=(GROUPS,),
        in_specs=[
            by_column,
            by_column,
            pl.BlockSpec((1, ROWS, 16), lambda s: (s, 0, 0)),
            pl.BlockSpec((1, 16, ROWS), lambda s: (s, 0, 0)),
            whole,
            whole,
        ],
        out_specs=[by_column, by_column, whole, whole],
        out_shape=[wide, wide, small, small],
        scratch_shapes=[pltpu.VMEM((ROWS, ROWS), F32), pltpu.VMEM((ROWS, ROWS), F32)],
        compiler_params=pltpu.CompilerParams(vmem_limit_bytes=40 << 20),
        cost_estimate=pl.CostEstimate(
            flops=20_000_000_000, bytes_accessed=12_000_000, transcendentals=3_000_000
        ),
        name="within_chunk",
    )(x, dy, cum, cumt, b, c)


CHIPS = 4
VMEM = pl.BlockSpec(memory_space=pltpu.VMEM)
SMEM = pl.BlockSpec(memory_space=pltpu.SMEM)
PAIR = (2, N, GC)
LOWS = 64


def on_chip(kernel, name, outs, *args, scratch=(), scalars=1):
    return pl.pallas_call(
        kernel,
        in_specs=[SMEM] * scalars + [VMEM] * (len(args) - scalars),
        out_specs=[VMEM] * len(outs),
        out_shape=outs,
        scratch_shapes=list(scratch),
        compiler_params=pltpu.CompilerParams(vmem_limit_bytes=44 << 20),
        name=name,
    )(*args)


def pack_kernel(ld_ref, gain_ref, out_ref):
    out_ref[...] = jnp.zeros_like(out_ref)
    for chunk in range(GROUPS):
        rows = ld_ref[:, chunk * ROWS : (chunk + 1) * ROWS]
        for core in range(2):
            at = 2 * (chunk // 2) + core
            out_ref[at, chunk % 2, 0:HG, :] = rows
            out_ref[at, chunk % 2, HG : HG + 1, 0:HG] = gain_ref[...]


def owner_kernel(ld_ref, out_ref):
    width = 2 * ROWS
    of = lax.broadcasted_iota(jnp.int32, (8, 8 * ROWS), 1) // width
    row = lax.broadcasted_iota(jnp.int32, (8, 8 * ROWS), 0)
    pick = jnp.logical_or(of == row, row == CHIPS).astype(BF16)
    totals = sum(dot(pick, part, NT) for part in thirds(ld_ref[...]))
    out_ref[...] = spread(jnp.exp(totals))


def decays_kernel(core_ref, got_ref, cumt_ref, cum_ref, gain_ref, kept_ref):
    low = core_ref[0] == 0
    t = lax.broadcasted_iota(jnp.int32, (ROWS, ROWS), 0)
    s = lax.broadcasted_iota(jnp.int32, (ROWS, ROWS), 1)
    upper = (t <= s).astype(BF16)
    lower = (t >= s).astype(BF16)
    is_head = lax.broadcasted_iota(jnp.int32, (GROUPS, 16, ROWS), 1) < HG
    flat, tall = [], []
    for half in range(2):
        ld = jnp.where(is_head, got_ref[:, half], 0.0).reshape(GROUPS * 16, ROWS)
        parts = thirds(ld)
        flat.append(sum(dot(part, upper) for part in parts))
        tall.append(sum(dot(lower, part, NT) for part in parts))
    cumt_ref[...] = jnp.where(low, flat[0], flat[1]).reshape(GROUPS, 16, ROWS)
    own = jnp.where(low, tall[0], tall[1])
    for g in range(GROUPS):
        cum_ref[g] = own[:, 16 * g : 16 * g + 16]
        gain_ref[g] = spread(got_ref[g, 0, HG : HG + 1, :])
    for half in range(2):
        ends = jnp.exp(tall[half][ROWS - 1 : ROWS, :])
        for j in range(CHIPS):
            a = ends[:, 32 * j : 32 * j + 16]
            b = ends[:, 32 * j + 16 : 32 * j + 32]
            kept_ref[half, j] = spread(jnp.where(low, a, b))


def states_kernel(place, x_ref, dy_ref, cum_ref, bt_ref, ct_ref, send_ref, keep_ref):
    low = place[0] == 0
    for way, (v_ref, m_ref) in enumerate(((x_ref, bt_ref), (dy_ref, ct_ref))):
        m = m_ref[...]
        states = []
        for k in range(2):
            cum = cum_ref[k]
            scale = jnp.exp(cum[ROWS - 1 : ROWS, :] - cum if way == 0 else cum)
            high, low_part = halves(v_ref[:, k * GC : (k + 1) * GC].astype(F32) * spread(scale))
            states.append(dot(m, high) + dot(m, low_part))
        keep_ref[0, way] = jnp.where(low, states[0], states[1])
        send_ref[0, way] = jnp.where(low, states[1], states[0])


def chunk_states(place, x, dy, cum, bt, ct):
    columns = pl.BlockSpec((ROWS, 2 * GC), lambda s, place: (0, s))
    whole = pl.BlockSpec((N, ROWS), lambda s, place: (0, 0))
    quad = pl.BlockSpec((1, *PAIR), lambda s, place: (s, 0, 0, 0))
    return pl.pallas_call(
        states_kernel,
        grid_spec=pltpu.PrefetchScalarGridSpec(
            num_scalar_prefetch=1,
            grid=(CHIPS,),
            in_specs=[
                columns,
                columns,
                pl.BlockSpec((2, ROWS, 16), lambda s, place: (s, 0, 0)),
                whole,
                whole,
            ],
            out_specs=[quad, quad],
        ),
        out_shape=[jax.ShapeDtypeStruct((CHIPS, *PAIR), F32)] * 2,
        compiler_params=pltpu.CompilerParams(vmem_limit_bytes=60 << 20),
        name="chunk_states",
    )(place, x, dy, cum, bt, ct)


def join_kernel(place_ref, keep_ref, come_ref, kept_ref, *outs):
    low = place_ref[0] == 0
    for turn, out in enumerate(outs):
        j = lax.rem(place_ref[1] + turn, CHIPS)
        for way in range(2):
            scaled = low if way == 0 else jnp.logical_not(low)
            keep, come = keep_ref[j, way], come_ref[j, way]
            out[way] = jnp.where(scaled, keep, come) * kept_ref[1 - way, j] + jnp.where(
                scaled, come, keep
            )


ORDERS = ((0, 1, 2, 3), (3, 2, 1, 0))


def totals_kernel(place_ref, r0, r1, r2, r3, d_ref, out_ref, sorted_ref):
    for turn, ref in enumerate((r0, r1, r2, r3)):
        sorted_ref[lax.rem(place_ref[1] - turn + CHIPS, CHIPS)] = ref[...]
    for way, order in enumerate(ORDERS):
        total = sorted_ref[order[0], way]
        for c in order[1:]:
            total = total * d_ref[c : c + 1, :] + sorted_ref[c, way]
        out_ref[16 * way : 16 * way + 16, :, :GC] = total.reshape(16, 8, GC)
    for tile in range(PAIRS):
        row = d_ref[CHIPS : CHIPS + 1, 128 * tile : 128 * tile + 128]
        out_ref[:, tile : tile + 1, GC:] = jnp.broadcast_to(row[None], (32, 1, 128))
    out_ref[:, PAIRS:, GC:] = jnp.zeros((32, 8 - PAIRS, 128), F32)


def chain_kernel(flag_ref, p_ref, out_ref):
    backward = flag_ref[0] == 1
    state = [jnp.zeros((8, 128), F32) for _ in range(PAIRS)]
    for s in range(32):
        k = jnp.where(backward, 31 - s, s)
        for t in range(PAIRS):
            columns = slice(128 * t, 128 * t + 128)
            out_ref[k, :, columns] = state[t]
            state[t] = state[t] * p_ref[k, t : t + 1, GC:] + p_ref[k, :, columns]


def entering_kernel(place_ref, sorted_ref, d_ref, edge_ref, o0, o1, o2, o3, all_ref):
    for way, order in enumerate(ORDERS):
        e = edge_ref[16 * way : 16 * way + 16].reshape(N, GC)
        for c in order:
            all_ref[c, way] = e
            if c != order[-1]:
                e = e * d_ref[c : c + 1, :] + sorted_ref[c, way]
    for turn, out in enumerate((o0, o1, o2, o3)):
        at = lax.rem(place_ref[1] + turn, CHIPS)
        for way in range(2):
            high, low = halves(all_ref[at, way])
            out[way, :N] = high
            out[way, N:] = low[:LOWS]


def fork_kernel(place_ref, r0, r1, r2, r3, keep_ref, come_ref, kept_ref, mine_ref, send_ref):
    low = place_ref[0] == 0
    for turn, ref in enumerate((r0, r1, r2, r3)):
        j = lax.rem(place_ref[1] - turn + CHIPS, CHIPS)
        for way in range(2):
            direct_is_mine = low if way == 0 else jnp.logical_not(low)
            low_rows = jnp.concatenate(
                [ref[way, N:].astype(F32), jnp.zeros((N - LOWS, GC), F32)], axis=0
            )
            direct = ref[way, :N].astype(F32) + low_rows
            passed = jnp.where(direct_is_mine, keep_ref[j, way], come_ref[j, way])
            through = kept_ref[way, j] * direct + passed
            mine_ref[j, way] = jnp.where(direct_is_mine, direct, through)
            send_ref[j, way] = jnp.where(direct_is_mine, through, direct)


def finish_kernel(
    place, x_ref, dy_ref, cum_ref, y_ref, dx_ref, mine_ref, come_ref, gain_ref, b_ref, c_ref,
    db0_ref, dc0_ref, out_ref, gs_ref, o0, o1, o2, o3, db_ref, dc_ref, gd_ref,
):
    step = pl.program_id(0)
    low_core = place[0] == 0

    @pl.when(step == 0)
    def _():
        db_ref[...] = db0_ref[...]
        dc_ref[...] = dc0_ref[...]

    def both(way):
        mine, come = mine_ref[0, way], come_ref[0, way]
        return jnp.concatenate([jnp.where(low_core, mine, come), jnp.where(low_core, come, mine)], axis=1)

    cums = cum_ref[0], cum_ref[1]
    from_start = jnp.concatenate([spread(jnp.exp(v)) for v in cums], axis=1)
    to_end = jnp.concatenate([spread(jnp.exp(v[ROWS - 1 : ROWS, :] - v)) for v in cums], axis=1)
    gain = jnp.concatenate([gain_ref[0], gain_ref[1]], axis=1)
    x = x_ref[...].astype(F32)
    dy = dy_ref[...].astype(F32)
    entering, leaving = both(0), both(1)
    b, c = b_ref[...], c_ref[...]

    def carried(matrix, state, scale, v):
        parts = jnp.concatenate(halves(state), axis=0)
        product = scale * dot(jnp.concatenate([matrix, matrix], axis=1), parts)
        high, low = halves(scale * v)
        wide = dot(high, parts, NT)
        return product, wide[:, :N] + wide[:, N:] + dot(low, parts[:N], NT)

    y_carried, dc = carried(c, entering, from_start, dy)
    dx_carried, db = carried(b, leaving, to_end, x)
    y = y_ref[...] + y_carried
    dx_in = dx_ref[...]
    out_ref[...] = (y + gain * x).astype(BF16)
    gs_ref[...] = (dx_in + dx_carried + gain * dy).astype(BF16)
    dc_ref[...] += dc
    db_ref[...] += db
    of_head = (
        lax.broadcasted_iota(jnp.int32, (32, 2 * GC), 1) // GC * 16
        + lax.broadcasted_iota(jnp.int32, (32, 2 * GC), 1) % GC // HEAD
        == lax.broadcasted_iota(jnp.int32, (32, 2 * GC), 0)
    ).astype(BF16)

    def by_head(v):
        high, low = halves(v)
        return dot(of_head, high, NT) + dot(of_head, low, NT)

    x_dx = x * dx_carried
    row = from_start[ROWS - 1 : ROWS, :] * jnp.sum(entering * leaving, axis=0, keepdims=True)
    row += jnp.sum(x_dx, axis=0, keepdims=True)
    t = lax.broadcasted_iota(jnp.int32, (ROWS, ROWS), 0)
    s = lax.broadcasted_iota(jnp.int32, (ROWS, ROWS), 1)
    after = (t >= s).astype(BF16)
    gd = jnp.broadcast_to(by_head(jnp.broadcast_to(row, (8, 2 * GC)))[:, 0:1], (32, ROWS))
    for part in thirds(by_head(dy * y - (x * dx_in + x_dx))):
        gd += dot(part, after)
    gd_ref[step] = gd

    @pl.when(step == CHIPS - 1)
    def _():
        for turn, out in enumerate((o0, o1, o2, o3)):
            out[0:ROWS, :] = db_ref[...]
            out[ROWS : 2 * ROWS, :] = dc_ref[...]
            mine = gd_ref[lax.rem(place[1] + turn, CHIPS)]
            out[384:416, :] = mine[:, 0:128]
            out[416:448, 0:64] = mine[:, 128:192]
            out[416:448, 64:128] = jnp.zeros((32, 64), F32)


def finish(place, x, dy, cum, y, dx, mine, come, gain, b, c, db, dc):
    columns = pl.BlockSpec((ROWS, 2 * GC), lambda s, place: (0, s))
    by_chip = lambda *shape: pl.BlockSpec((2, *shape), lambda s, place: (s, 0, 0))
    quad = pl.BlockSpec((1, *PAIR), lambda s, place: (s, 0, 0, 0))
    whole = lambda *shape: pl.BlockSpec(shape, lambda s, place: (0, 0))
    wide = jax.ShapeDtypeStruct((ROWS, GC * GROUPS), BF16)
    return pl.pallas_call(
        finish_kernel,
        grid_spec=pltpu.PrefetchScalarGridSpec(
            num_scalar_prefetch=1,
            grid=(CHIPS,),
            in_specs=[
                columns, columns, by_chip(ROWS, 16), columns, columns, quad, quad,
                by_chip(1, GC), *[whole(ROWS, N)] * 4,
            ],
            out_specs=[columns, columns] + [whole(448, 128)] * 4,
            scratch_shapes=[
                pltpu.VMEM((ROWS, N), F32), pltpu.VMEM((ROWS, N), F32), pltpu.VMEM((CHIPS, 32, ROWS), F32),
            ],
        ),
        out_shape=[wide, wide] + [jax.ShapeDtypeStruct((448, 128), F32)] * 4,
        compiler_params=pltpu.CompilerParams(vmem_limit_bytes=57 << 20),
        name="finish",
    )(place, x, dy, cum, y, dx, mine, come, gain, b, c, db, dc)


def tie(*values):
    return lax.optimization_barrier(values)


def turned(v):
    r = {
        turn: lax.ppermute(v[turn], "y", [(i, (i + turn) % CHIPS) for i in range(CHIPS)])
        for turn in (2, 1, 3)
    }
    return [v[0], r[1], r[2], r[3]]


def gathered(parts, iy, low):
    by_chip = jnp.roll(jnp.stack([parts[0], parts[3], parts[2], parts[1]]), iy, axis=0)
    other = lax.ppermute(by_chip, "core", SWAP)
    return jnp.stack(
        [jnp.where(low, by_chip, other), jnp.where(low, other, by_chip)], axis=1
    ).reshape(GROUPS, *by_chip.shape[1:])


def shards(x, dy, b_all, c_all, log_decay, skip_gain):
    ix = lax.axis_index("x")
    iy, core = lax.axis_index("y"), lax.axis_index("core")
    place = jnp.stack([core, iy]).astype(jnp.int32)
    row0 = (2 * iy + core) * ROWS
    b = lax.dynamic_slice_in_dim(b_all, row0, ROWS, 0)
    c = lax.dynamic_slice_in_dim(c_all, row0, ROWS, 0)
    swap = lambda v: lax.ppermute(v, "core", SWAP)
    over_ctx = lambda v: lax.all_to_all(v, ("x", "z"), split_axis=0, concat_axis=0, tiled=True)
    pair = lambda dtype: jax.ShapeDtypeStruct(PAIR, dtype)
    quad = jax.ShapeDtypeStruct((CHIPS, *PAIR), F32)

    ldt = log_decay.T
    [packed] = on_chip(
        pack_kernel, "pack", [jax.ShapeDtypeStruct((GROUPS, 2, 16, ROWS), F32)],
        ldt, skip_gain.reshape(1, HG), scalars=0,
    )
    got = lax.all_to_all(packed, ("y", "core"), split_axis=0, concat_axis=0, tiled=True)
    cumt, cum, gain, kept = on_chip(
        decays_kernel, "decays",
        [
            jax.ShapeDtypeStruct((GROUPS, 16, ROWS), F32),
            jax.ShapeDtypeStruct((GROUPS, ROWS, 16), F32),
            jax.ShapeDtypeStruct((GROUPS, 1, GC), F32),
            jax.ShapeDtypeStruct((2, CHIPS, 1, GC), F32),
        ],
        place, got,
    )
    send, keep = chunk_states(place, x, dy, cum, b.T, c.T)
    come = swap(send)
    out = on_chip(join_kernel, "join", [pair(F32)] * 4, place, keep, come, kept)
    parts = turned(out)
    x_w, dy_w, ldt_w, _ = tie(x, dy, ldt, out[0])
    [own] = on_chip(owner_kernel, "owner_decays", [jax.ShapeDtypeStruct((8, GC), F32)], ldt_w, scalars=0)
    inside = within(x_w, dy_w, cum, cumt, b, c)
    y_in, dx_in, db_in, dc_in, *parts = tie(*inside, *parts)
    total, by_chip = on_chip(
        totals_kernel, "totals", [jax.ShapeDtypeStruct((32, 8, GC + 128), F32), quad], place, *parts, own
    )
    total = over_ctx(total)
    flag = (ix >= 2).reshape(1).astype(jnp.int32)
    [edge] = on_chip(
        chain_kernel, "chain", [jax.ShapeDtypeStruct((32, 8, GC), F32)], flag, total
    )
    edge = over_ctx(edge)
    out = on_chip(
        entering_kernel, "entering", [jax.ShapeDtypeStruct((2, N + LOWS, GC), BF16)] * 4, place, by_chip, own, edge,
        scratch=[pltpu.VMEM((CHIPS, *PAIR), F32)],
    )
    mine, send = on_chip(fork_kernel, "fork", [quad] * 2, place, *turned(out), keep, come, kept)
    scan_out, grad_x, *ends = finish(
        place, x, dy, cum, y_in, dx_in, mine, swap(send), gain, b, c, db_in, dc_in
    )
    ends = gathered(turned(ends), iy, core == 0)
    grad_b = ends[:, :ROWS].reshape(GROUPS * ROWS, N)
    grad_c = ends[:, ROWS : 2 * ROWS].reshape(GROUPS * ROWS, N)
    rest = ends[:, 2 * ROWS :].reshape(GROUPS, 2, 2, 16, 128)
    rest = lax.dynamic_index_in_dim(rest, core, 2, keepdims=False)
    rest = jnp.concatenate([rest[:, 0, :HG], rest[:, 1, :HG, :64]], axis=2)
    grad_decay = rest.transpose(0, 2, 1).reshape(GROUPS * ROWS, HG)
    return scan_out, grad_x, grad_b, grad_c, grad_decay


def solution(mesh):
    grid = Mesh(mesh.devices.reshape(4, 8, 4, 2), ("x", "z", "y", "core"))
    ctx, head = ("x", "z"), ("y", "core")
    rows = P((*ctx, *head), None)
    return jax.shard_map(
        shards,
        mesh=grid,
        in_specs=(rows, rows, P(ctx, None), P(ctx, None), P(ctx, head), P(head)),
        out_specs=(rows, rows, P(ctx, None), P(ctx, None), P(ctx, head)),
        check_vma=False,
    )
```
